256 devices in a mesh: band: 64 (over y, z, x_lo), grid: 4 (over x_hi, core).
Axes of the slice: x: 4 (x_hi: 2, x_lo: 2; x = x_hi * 2 + x_lo), y: 4, z: 8, core: 2. Of those that a mesh axis runs over, the one named last changes fastest.
Arguments:
- orbitals: bfloat16 [256, 48, 2304], P('band', 'grid'), may hold values from -6 to 6
Outputs:
- exchange: float32 [256, 48, 2304], P('band', 'grid')
The draws below stay inside these ranges and needn't reach their ends.
All inputs are finite; a program needn't handle non-finite values.
Results may differ from the reference program's by a relative error of at most 0.0003.
Values may be sent and summed in bfloat16 or wider, within the bound.
A program may use at most 64 MiB of HBM per device.

```python
import math
import jax
import jax.numpy as jnp
from jax import lax

POINTS = 48
ORB_DEV = 4
STEPS = 2
ORBITALS = 256
N_BAND = 64


def level_of(stream_key, shape, cuts, least, top_value):
    factor_of = 1.0
    for dim, parts in cuts:
        draws = jax.random.uniform(jax.random.fold_in(jax.random.fold_in(stream_key, 6), dim), (parts,), jnp.float32, least / len(cuts), top_value / len(cuts))
        factor_of = factor_of * jnp.repeat(jnp.exp(draws), shape[dim] // parts).reshape((-1,) + (1,) * (len(shape) - 1 - dim))
    return factor_of


def noise(stream_key, dims, deviation, reach, cuts=(), held_as=jnp.bfloat16):
    values = deviation * jax.random.normal(stream_key, dims, jnp.float32)
    if cuts:
        values = values * level_of(stream_key, dims, cuts, -0.22, 0.18)
    return jnp.clip(values, -reach, reach).astype(held_as)


def setup_inputs(seed: int = 0) -> dict:
    splits = jax.random.split(jax.random.key(seed), 2)
    return {
        "orbitals": noise(splits[0], (ORBITALS, POINTS, POINTS * POINTS), 1.0, 6.0, ((0, 64), (1, 4))),
    }


BOX = 37.25
OMEGA = 0.106
MIXING = 0.25


def screened_kernel(points):
    positions = jnp.arange(points, dtype=jnp.int32)
    wavenumber = ((positions + points // 2) % points - points // 2).astype(jnp.float32) * (2.0 * math.pi / BOX)
    squares = wavenumber[:, None, None] ** 2 + wavenumber[None, :, None] ** 2 + wavenumber[None, None, :] ** 2
    bounded = jnp.where(squares > 0.0, squares, jnp.float32(1.0))
    screened = 4.0 * math.pi / bounded * (1.0 - jnp.exp(-bounded / (4.0 * OMEGA * OMEGA)))
    return jnp.where(squares > 0.0, screened, jnp.float32(math.pi / (OMEGA * OMEGA)))


def pair_potentials(first_block, second_block, kernel):
    density = first_block[:, None].astype(jnp.float32) * second_block[None, :].astype(jnp.float32)
    spectrum = jnp.fft.fftn(density, axes=(2, 3, 4))
    return jnp.real(jnp.fft.ifftn(spectrum * kernel, axes=(2, 3, 4))).astype(jnp.float32)


def reference(orbitals):
    points = orbitals.shape[1]
    groups = orbitals.reshape(N_BAND, ORB_DEV, points, points, points)
    kernel = screened_kernel(points)
    combined = jnp.zeros(groups.shape, jnp.float32)
    for distance in range(1, STEPS + 1):
        partner = jnp.roll(groups, distance, axis=0)

        def one_group(pairing):
            home_block, other_block = pairing
            potential = pair_potentials(home_block, other_block, kernel)
            to_home = jnp.sum(potential * other_block[None].astype(jnp.float32), axis=1)
            to_other = jnp.sum(potential * home_block[:, None].astype(jnp.float32), axis=0)
            return to_home, to_other

        to_home, to_other = lax.map(one_group, (groups, partner))
        combined = combined + to_home + jnp.roll(to_other, -distance, axis=0)
    return (-MIXING * combined).reshape(orbitals.shape)
```

```python
import math

import jax
import jax.numpy as jnp
import ml_dtypes
import numpy as np
from jax import lax
from jax.experimental import pallas as pl
from jax.experimental.pallas import tpu as pltpu
from jax.sharding import PartitionSpec as P

POINTS = 48
PLANE = POINTS * POINTS
GROUP = 4
SLAB = 12
BAND = 64
CHUNK = 384
BOX = 37.25
OMEGA = 0.106
MIXING = 0.25
ROWS = 4 * GROUP * SLAB
CLASSES = ((0, 384), (384, 384), (768, 768), (1536, 768))


def halves(table):
    high = table.astype(ml_dtypes.bfloat16)
    low = (table - high.astype(np.float64)).astype(ml_dtypes.bfloat16)
    return high, low


def tables():
    index = np.arange(POINTS)
    angles = 2.0 * np.pi * (np.outer(index, index) % POINTS) / POINTS
    cas = np.cos(angles) + np.sin(angles)

    def spread(weights):
        rows = np.zeros((8, POINTS))
        for fine in range(8):
            rows[fine, fine::8] = weights
        return rows

    even, odd = [1, 1, 1, 1, 1, 1], [1, -1, 1, -1, 1, -1]
    real2, imag2 = [1, -0.5, -0.5, 1, -0.5, -0.5], [0, 1, -1, 0, 1, -1]
    real1, imag1 = [1, 0.5, -0.5, -1, -0.5, 0.5], [0, 1, 1, 0, -1, -1]
    matrices, order = [], []
    for parts, residues in (
        ((even,), (0,)),
        ((odd,), (3,)),
        ((real2, imag2), (2, 4)),
        ((real1, imag1), (1, 5)),
    ):
        folded = np.concatenate([spread(part) for part in parts])
        waves = [k for k in range(POINTS) if k % 6 in residues]
        small = cas[waves] @ folded.T @ np.linalg.inv(folded @ folded.T)
        matrices.append(np.kron(small, cas))
        order += waves
    signed = ((index + POINTS // 2) % POINTS - POINTS // 2) * (2.0 * np.pi / BOX)
    along_y, along_z = np.repeat(np.array(order), POINTS), np.tile(index, POINTS)
    squares = (
        signed[:, None] ** 2 + signed[along_y][None] ** 2 + signed[along_z][None] ** 2
    )
    bounded = np.where(squares > 0.0, squares, 1.0)
    screened = 4.0 * np.pi / bounded * (1.0 - np.exp(-bounded / (4.0 * OMEGA * OMEGA)))
    screened = np.where(squares > 0.0, screened, np.pi / (OMEGA * OMEGA)) / POINTS**3

    forward = [halves(m.T) for m in matrices]
    inverse = [halves(m) for m in matrices]
    small = np.stack([np.stack([w[c][p] for c in (0, 1) for p in (0, 1)]) for w in (forward, inverse)])
    large = np.stack([np.stack([w[c][p] for c in (2, 3) for p in (0, 1)]) for w in (forward, inverse)])

    first, second = [], []
    for device in range(4):
        matrix = np.zeros((GROUP, POINTS, 4, GROUP, SLAB))
        for slot in range(4):
            base = SLAB * (device ^ slot)
            for orbital in range(GROUP):
                matrix[orbital, :, slot, orbital, :] = cas[:, base : base + SLAB]
        matrix = matrix.reshape(ROWS, ROWS)
        for source, out in ((matrix, first), (matrix.T, second)):
            high, low = halves(source)
            out.append(np.concatenate([high, low, high], axis=1))
    along_x = np.stack([np.stack(first), np.stack(second)], axis=1)
    return small, large, along_x, screened.astype(np.float32)


def parted(value):
    high = value.astype(jnp.bfloat16)
    return high, (value - high.astype(jnp.float32)).astype(jnp.bfloat16)


def dot(left, right):
    return jnp.dot(left, right, preferred_element_type=jnp.float32)


def fold(d):
    s = [d[p] + d[p + 3] for p in range(3)]
    t = [d[p] - d[p + 3] for p in range(3)]
    u, v = s[1] + s[2], t[1] - t[2]
    return (s[0] + u, t[0] - v, s[0] - 0.5 * u, s[1] - s[2], t[0] + 0.5 * v, t[1] + t[2])


def unfold(f):
    z0, z3, r2, i2, r1, i1 = f
    a, b = z0 - 0.5 * r2, z3 - 0.5 * r1
    s = (z0 + r2, a + i2, a - i2)
    t = (z3 + r1, i1 - b, i1 + b)
    return [s[p] + t[p] for p in range(3)] + [s[p] - t[p] for p in range(3)]


def densities(slots, home_in, wide, z_hi, z_lo):
    for q in slots:
        for r in range(0, POINTS, 16):
            for tile in range(3):
                d = []
                for p in range(6):
                    lanes = pl.ds(p * CHUNK + tile * 128, 128)
                    rows = pl.ds(r, 16)
                    d.append(home_in[q, rows, lanes].astype(jnp.float32) * wide[q, rows, lanes])
                for p, value in enumerate(fold(d)):
                    high, low = parted(value)
                    at = (pl.ds(q * POINTS + r, 16), pl.ds(p * CHUNK + tile * 128, 128))
                    z_hi[at] = high
                    z_lo[at] = low


def weights(small, large, which, cls):
    return (small, large)[cls // 2], which, 2 * (cls % 2)


def plane(rows, cls, source, table):
    high, low = source
    ref, which, base = table
    first, lanes = CLASSES[cls]
    at = (pl.ds(rows[0], rows[1]), pl.ds(first, lanes))
    left = jnp.concatenate([high[at], high[at], low[at]], axis=1)
    w_hi, w_lo = ref[which, base], ref[which, base + 1]
    return dot(left, jnp.concatenate([w_hi, w_lo, w_hi], axis=0))


def middle(cls, s, u, along_x, screened):
    first, lanes = CLASSES[cls]
    for start in range(first, first + lanes, CHUNK):
        at = (slice(None), pl.ds(start, CHUNK))
        s_hi, s_lo = s[0][at], s[1][at]
        spectrum = dot(along_x[0], jnp.concatenate([s_hi, s_hi, s_lo], axis=0))
        table = screened[at]
        weighted = spectrum * jnp.concatenate([table] * GROUP, axis=0)
        t_hi, t_lo = parted(weighted)
        back = dot(along_x[1], jnp.concatenate([t_hi, t_hi, t_lo], axis=0))
        u[0][at], u[1][at] = parted(back)


def products(q, last, home_in, wide, g, home_sum, vis_sum):
    for tile in range(3):
        f = []
        for p in range(6):
            f.append(g[pl.ds(q * POINTS, POINTS), pl.ds(p * CHUNK + tile * 128, 128)])
        for p, value in enumerate(unfold(f)):
            column = p * CHUNK + tile * 128
            lanes = pl.ds(column, 128)
            home = value * wide[q, :, lanes]
            if last:
                home = home + home_sum[q, :, lanes]
            home_sum[q, :, lanes] = home
            other = value * home_in[q, :, lanes].astype(jnp.float32)
            other = other[:24] + other[24:]
            other = other[:SLAB] + other[SLAB:]
            half = column // 1152
            vis_sum[q, pl.ds(SLAB * half, SLAB), pl.ds(column - 1152 * half, 128)] = other


def kernel(
    orbitals, packed, small_hbm, large_hbm, along_hbm, screened_hbm, out,
    home_in, vis_in, wide, z_hi, z_lo, s_hi, s_lo, g,
    home_sum, vis_sum, sib_relay, sib_final, far_out, far_in, vis_back,
    small, large, along_x, screened,
    table_sem, own_sem, home_send, home_recv, vis_send, vis_recv,
    sum_send, sum_recv, back_send, back_recv,
):
    band, me = lax.axis_index("band"), lax.axis_index("grid")

    def partner(bit):
        return me + bit - 2 * bit * (lax.rem(me // bit, 2))

    def group(distance):
        return lax.rem(band + distance + BAND, BAND)

    sibling, far = (band, partner(1)), (band, partner(2))

    barrier = pltpu.get_barrier_semaphore()
    pl.semaphore_signal(barrier, 1, device_id=sibling)
    pl.semaphore_signal(barrier, 1, device_id=far)
    for distance in (-2, -1, 1, 2):
        for j in range(4):
            pl.semaphore_signal(barrier, 1, device_id=(group(distance), j))

    own = pltpu.make_async_copy(packed, home_in.at[0], own_sem)
    own.start()
    loads = [
        pltpu.make_async_copy(small_hbm, small, table_sem.at[0]),
        pltpu.make_async_copy(large_hbm, large, table_sem.at[1]),
        pltpu.make_async_copy(along_hbm.at[me], along_x, table_sem.at[2]),
        pltpu.make_async_copy(screened_hbm, screened, table_sem.at[3]),
    ]
    for load in loads:
        load.start()
    pl.semaphore_wait(barrier, 18)

    def home_copy(source, slot, target):
        return pltpu.make_async_remote_copy(
            source, home_in.at[slot], home_send.at[slot], home_recv.at[slot], device_id=target
        )

    def xor(a, j):
        low = lax.rem(a + j, 2)
        high = lax.rem(a // 2 + j // 2, 2)
        return 2 * high + low

    far_copy = home_copy(packed, 2, far)
    far_copy.start()
    sib_copy = home_copy(packed, 1, sibling)
    sib_copy.start()
    vis_copies = []
    for s in (1, 0):
        for j in range(4):
            copy = pltpu.make_async_remote_copy(
                orbitals.at[j],
                vis_in.at[s, xor(me, j)],
                vis_send.at[s, j],
                vis_recv.at[s, xor(me, j)],
                device_id=(group(s + 1), j),
            )
            copy.start()
            vis_copies.append(copy)

    def widen(s, slots):
        for q in slots:
            pltpu.make_async_remote_copy(
                orbitals.at[0], vis_in.at[s, q], vis_send.at[s, 0], vis_recv.at[s, q],
                device_id=sibling,
            ).wait_recv()
            value = vis_in[s, q].astype(jnp.float32)
            for i in range(GROUP):
                wide[s, q, pl.ds(SLAB * i, SLAB), :] = value

    def forward(s, rows):
        for cls in range(4):
            first, lanes = CLASSES[cls]
            value = plane(rows, cls, (z_hi, z_lo), weights(small, large, 0, cls))
            at = (pl.ds(rows[0], rows[1]), pl.ds(first, lanes))
            s_hi[at], s_lo[at] = parted(value)

    def backward(rows):
        for cls in range(4):
            first, lanes = CLASSES[cls]
            value = plane(rows, cls, (s_hi, s_lo), weights(small, large, 1, cls))
            g[pl.ds(rows[0], rows[1]), pl.ds(first, lanes)] = value

    own.wait()
    sib_copy.wait_recv()
    widen(1, (0, 1))
    densities((0, 1), home_in, wide.at[1], z_hi, z_lo)
    for load in loads:
        load.wait()
    forward(1, (0, 96))
    far_copy.wait_recv()
    relay = home_copy(home_in.at[2], 3, sibling)
    relay.start()
    widen(1, (2, 3))
    densities((2,), home_in, wide.at[1], z_hi, z_lo)
    relay.wait_recv()
    densities((3,), home_in, wide.at[1], z_hi, z_lo)
    forward(1, (96, 96))
    for cls in range(4):
        middle(cls, (s_hi, s_lo), (s_hi, s_lo), along_x, screened)
    backward((0, ROWS))
    for q in range(4):
        products(q, False, home_in, wide.at[1], g, home_sum, vis_sum.at[1])

    def send_back(s, q):
        copy = pltpu.make_async_remote_copy(
            vis_sum.at[s, q],
            vis_back.at[s, me],
            back_send.at[s, q],
            back_recv.at[s, me],
            device_id=(group(-s - 1), xor(me, q)),
        )
        copy.start()
        return copy

    back_copies = [send_back(1, q) for q in range(4)]

    widen(0, range(4))
    densities(range(4), home_in, wide.at[0], z_hi, z_lo)
    forward(0, (0, ROWS))
    for cls in range(4):
        middle(cls, (s_hi, s_lo), (s_hi, s_lo), along_x, screened)

    def sum_copy(source, target_ref, slot, target):
        return pltpu.make_async_remote_copy(
            source, target_ref, sum_send.at[slot], sum_recv.at[slot], device_id=target
        )

    backward((96, 96))
    products(3, True, home_in, wide.at[0], g, home_sum, vis_sum.at[0])
    to_relay = sum_copy(home_sum.at[3], sib_relay, 0, sibling)
    to_relay.start()
    products(2, True, home_in, wide.at[0], g, home_sum, vis_sum.at[0])
    back_copies += [send_back(0, 3), send_back(0, 2)]
    to_relay.wait_recv()
    far_out[...] = home_sum[2] + sib_relay[...]
    to_far = sum_copy(far_out, far_in, 1, far)
    to_far.start()
    backward((0, 96))
    products(1, True, home_in, wide.at[0], g, home_sum, vis_sum.at[0])
    to_final = sum_copy(home_sum.at[1], sib_final, 2, sibling)
    to_final.start()
    products(0, True, home_in, wide.at[0], g, home_sum, vis_sum.at[0])
    back_copies += [send_back(0, 1), send_back(0, 0)]

    to_final.wait_recv()
    for s in (1, 0):
        for j in range(4):
            pltpu.make_async_remote_copy(
                vis_sum.at[s, 0], vis_back.at[s, j], back_send.at[s, 0], back_recv.at[s, j],
                device_id=sibling,
            ).wait_recv()
    to_far.wait_recv()
    for i in range(GROUP):
        rows = pl.ds(SLAB * i, SLAB)
        for half in range(2):
            lanes = pl.ds(1152 * half, 1152)
            part = pl.ds(SLAB * half, SLAB)
            total = home_sum[0, rows, lanes] + sib_final[rows, lanes] + far_in[rows, lanes]
            total = total + (vis_back[0, i, part, :] + vis_back[1, i, part, :])
            out[i, :, lanes] = -MIXING * total

    for copy in [far_copy, sib_copy, relay, to_relay, to_far, to_final] + vis_copies + back_copies:
        copy.wait_send()


def solution(mesh):
    small, large, along_x, screened = tables()
    any_space = pl.BlockSpec(memory_space=pl.ANY)
    bf16, f32 = jnp.bfloat16, jnp.float32
    dma = pltpu.SemaphoreType.DMA
    call = pl.pallas_call(
        kernel,
        out_shape=jax.ShapeDtypeStruct((GROUP, SLAB, PLANE), f32),
        in_specs=[any_space] * 6,
        out_specs=pl.BlockSpec(memory_space=pltpu.VMEM),
        scratch_shapes=[
            pltpu.VMEM((4, POINTS, PLANE), bf16),
            pltpu.VMEM((2, 4, SLAB, PLANE), bf16),
            pltpu.VMEM((2, 4, POINTS, PLANE), f32),
            pltpu.VMEM((ROWS, PLANE), bf16),
            pltpu.VMEM((ROWS, PLANE), bf16),
            pltpu.VMEM((ROWS, PLANE), bf16),
            pltpu.VMEM((ROWS, PLANE), bf16),
            pltpu.VMEM((ROWS, PLANE), f32),
            pltpu.VMEM((4, POINTS, PLANE), f32),
            pltpu.VMEM((2, 4, 24, PLANE // 2), f32),
            pltpu.VMEM((POINTS, PLANE), f32),
            pltpu.VMEM((POINTS, PLANE), f32),
            pltpu.VMEM((POINTS, PLANE), f32),
            pltpu.VMEM((POINTS, PLANE), f32),
            pltpu.VMEM((2, 4, 24, PLANE // 2), f32),
            pltpu.VMEM(small.shape, bf16),
            pltpu.VMEM(large.shape, bf16),
            pltpu.VMEM(along_x.shape[1:], bf16),
            pltpu.VMEM(screened.shape, f32),
            dma((4,)), dma, dma((4,)), dma((4,)), dma((2, 4)), dma((2, 4)),
            dma((3,)), dma((3,)), dma((2, 4)), dma((2, 4)),
        ],
        compiler_params=pltpu.CompilerParams(
            collective_id=0, has_side_effects=True, vmem_limit_bytes=60 << 20
        ),
    )

    def body(orbitals):
        packed = orbitals.reshape(GROUP * SLAB, PLANE)
        return call(orbitals, packed, small, large, along_x, screened)

    placed = P("band", "grid", None)
    return jax.shard_map(
        body, mesh=mesh, in_specs=(placed,), out_specs=placed, check_vma=False
    )
```

```python
import functools

import jax
import jax.numpy as jnp
import ml_dtypes
import numpy as np
from jax import lax
from jax.experimental import pallas as pl
from jax.experimental.pallas import tpu as pltpu
from jax.sharding import PartitionSpec as P

POINTS = 48
PLANE = POINTS * POINTS
GROUP = 4
SLAB = 12
BAND = 64
CHUNK = 384
BOX = 37.25
OMEGA = 0.106
MIXING = 0.25
ROWS = 4 * GROUP * SLAB
HALF = ROWS // 2
CLASSES = ((0, 384), (384, 384), (768, 768), (1536, 768))


def halves(table):
    high = table.astype(ml_dtypes.bfloat16)
    low = (table - high.astype(np.float64)).astype(ml_dtypes.bfloat16)
    return high, low


def tables():
    index = np.arange(POINTS)
    angles = 2.0 * np.pi * (np.outer(index, index) % POINTS) / POINTS
    cas = np.cos(angles) + np.sin(angles)

    def spread(weights):
        rows = np.zeros((8, POINTS))
        for fine in range(8):
            rows[fine, fine::8] = weights
        return rows

    even, odd = [1, 1, 1, 1, 1, 1], [1, -1, 1, -1, 1, -1]
    real2, imag2 = [1, -0.5, -0.5, 1, -0.5, -0.5], [0, 1, -1, 0, 1, -1]
    real1, imag1 = [1, 0.5, -0.5, -1, -0.5, 0.5], [0, 1, 1, 0, -1, -1]
    matrices, order = [], []
    for parts, residues in (
        ((even,), (0,)),
        ((odd,), (3,)),
        ((real2, imag2), (2, 4)),
        ((real1, imag1), (1, 5)),
    ):
        folded = np.concatenate([spread(part) for part in parts])
        waves = [k for k in range(POINTS) if k % 6 in residues]
        small = cas[waves] @ folded.T @ np.linalg.inv(folded @ folded.T)
        matrices.append(np.kron(small, cas))
        order += waves
    signed = ((index + POINTS // 2) % POINTS - POINTS // 2) * (2.0 * np.pi / BOX)
    along_y, along_z = np.repeat(np.array(order), POINTS), np.tile(index, POINTS)
    squares = (
        signed[:, None] ** 2 + signed[along_y][None] ** 2 + signed[along_z][None] ** 2
    )
    bounded = np.where(squares > 0.0, squares, 1.0)
    screened = 4.0 * np.pi / bounded * (1.0 - np.exp(-bounded / (4.0 * OMEGA * OMEGA)))
    screened = np.where(squares > 0.0, screened, np.pi / (OMEGA * OMEGA)) / POINTS**3

    forward = [halves(m.T) for m in matrices]
    inverse = [halves(m) for m in matrices]
    small = np.stack([np.stack([w[c][p] for c in (0, 1) for p in (0, 1)]) for w in (forward, inverse)])
    large = np.stack([np.stack([w[c][p] for c in (2, 3) for p in (0, 1)]) for w in (forward, inverse)])

    along = []
    for device in range(4):
        matrix = np.zeros((2, POINTS, 4, 2, SLAB))
        for slot in range(4):
            base = SLAB * (device ^ slot)
            for orbital in range(2):
                matrix[orbital, :, slot, orbital, :] = cas[:, base : base + SLAB]
        matrix = matrix.reshape(HALF, HALF)
        for source in (matrix, matrix.T):
            high, low = halves(source)
            top = np.concatenate([high, high], axis=1)
            bottom = np.concatenate([low, np.zeros_like(low)], axis=1)
            along.append(np.concatenate([top, bottom], axis=0))
    along_x = np.stack(along).reshape(4, 2, ROWS, ROWS)
    return small, large, along_x, screened.astype(np.float32)


def parted(value):
    high = value.astype(jnp.bfloat16)
    return high, (value - high.astype(jnp.float32)).astype(jnp.bfloat16)


def dot(left, right):
    return jnp.dot(left, right, preferred_element_type=jnp.float32)


def fold(d):
    s = [d[p] + d[p + 3] for p in range(3)]
    t = [d[p] - d[p + 3] for p in range(3)]
    u, v = s[1] + s[2], t[1] - t[2]
    return (s[0] + u, t[0] - v, s[0] - 0.5 * u, s[1] - s[2], t[0] + 0.5 * v, t[1] + t[2])


def unfold(f):
    z0, z3, r2, i2, r1, i1 = f
    a, b = z0 - 0.5 * r2, z3 - 0.5 * r1
    s = (z0 + r2, a + i2, a - i2)
    t = (z3 + r1, i1 - b, i1 + b)
    return [s[p] + t[p] for p in range(3)] + [s[p] - t[p] for p in range(3)]


def densities(pair, home_in, wide, z_hi, z_lo):
    for tile in range(3):
        d = []
        for p in range(6):
            lanes = pl.ds(p * CHUNK + tile * 128, 128)
            d.append([home_in[2 * pair + k, :, lanes].astype(jnp.float32) * wide[2 * pair + k, :, lanes] for k in range(2)])
        for two in range(2):
            rows = slice(24 * two, 24 * two + 24)
            parts = [jnp.concatenate([value[rows] for value in values], axis=0) for values in d]
            for p, value in enumerate(fold(parts)):
                at = (pl.ds(HALF * two + POINTS * pair, POINTS), pl.ds(p * CHUNK + tile * 128, 128))
                z_hi[at], z_lo[at] = parted(value)


def weights(small, large, which, cls):
    return (small, large)[cls // 2], which, 2 * (cls % 2)


def segments(pairs):
    return [HALF * two + POINTS * pair for two in range(2) for pair in pairs]


def plane(pairs, cls, source, table):
    ref, which, base = table
    first, lanes = CLASSES[cls]
    high, low = (
        jnp.concatenate([part[pl.ds(row, POINTS), pl.ds(first, lanes)] for row in segments(pairs)], axis=0)
        for part in source
    )
    count = high.shape[0]
    both = dot(jnp.concatenate([high, low], axis=0), ref[which, base])
    return both[:count] + both[count:] + dot(high, ref[which, base + 1])


def middle(start, s, u, along_x, screened):
    lanes = pl.ds(start, 768)
    table = screened[:, lanes]
    for two in range(2):
        at = (pl.ds(HALF * two, HALF), lanes)
        both = dot(along_x[0], jnp.concatenate([s[0][at], s[1][at]], axis=0))
        weighted = (both[:HALF] + both[HALF:]) * jnp.concatenate([table] * 2, axis=0)
        both = dot(along_x[1], jnp.concatenate(parted(weighted), axis=0))
        u[0][at], u[1][at] = parted(both[:HALF] + both[HALF:])


def products(q, last, home_in, wide, g, home_sum, vis_sum):
    for tile in range(3):
        f = []
        for p in range(6):
            lanes = pl.ds(p * CHUNK + tile * 128, 128)
            f.append(jnp.concatenate([g[pl.ds(HALF * two + 24 * q, 24), lanes] for two in range(2)], axis=0))
        for p, value in enumerate(unfold(f)):
            column = p * CHUNK + tile * 128
            lanes = pl.ds(column, 128)
            home = value * wide[q, :, lanes]
            if last:
                home = home + home_sum[q, :, lanes]
            home_sum[q, :, lanes] = home
            other = value * home_in[q, :, lanes].astype(jnp.float32)
            other = other[:24] + other[24:]
            other = other[:SLAB] + other[SLAB:]
            part, place = divmod(column // 128, 5)
            vis_sum[q, pl.ds(SLAB * part, SLAB), pl.ds(128 * place, 128)] = other


def scale_of(values):
    top = functools.reduce(jnp.maximum, [jnp.max(jnp.abs(v), axis=0, keepdims=True) for v in values])
    top = jnp.max(top, axis=1, keepdims=True)
    return (220.0 / jnp.maximum(top, 1e-30)).astype(jnp.bfloat16).astype(jnp.float32)


def coded(value, scale):
    power = value * scale
    for _ in range(4):
        power = power * power
    return jnp.where(value < 0.0, -power, power).astype(jnp.bfloat16)


def decoded(code, inverse):
    power = code.astype(jnp.float32)
    value = jnp.exp2(jnp.log2(jnp.abs(power)) * 0.0625) * inverse
    return jnp.where(power < 0.0, -value, value)


def code_visitor(source, target):
    tiles = [source[:, pl.ds(128 * k, 128)] for k in range(5)]
    scale = scale_of(tiles)
    spare = lax.broadcasted_iota(jnp.int32, (POINTS, 128), 0) >= 3 * SLAB
    for k in range(5):
        code = coded(tiles[k], scale)
        if k >= 3:
            code = jnp.where(spare, jnp.broadcast_to(scale, (POINTS, 128)), code.astype(jnp.float32))
        target[:, pl.ds(128 * k, 128)] = code.astype(jnp.bfloat16)


def kernel(
    arrived, small_hbm, large_hbm, along_hbm, screened_hbm, out,
    spread_rows, orbitals, home_in, vis_in, wide, z_hi, z_lo, s_hi, s_lo, g,
    home_sum, vis_sum, vis_code, sib_relay, sib_final, far_sum, far_out, far_in, vis_back,
    small, large, along_x, screened,
    table_sem, home_send, home_recv, vis_send, vis_recv,
    sum_send, sum_recv, back_send, back_recv,
):
    band, me = lax.axis_index("band"), lax.axis_index("grid")

    def partner(bit):
        return me + bit - 2 * bit * (lax.rem(me // bit, 2))

    def group(distance):
        return lax.rem(band + distance + BAND, BAND)

    sibling, far = (band, partner(1)), (band, partner(2))

    barrier = pltpu.get_barrier_semaphore()
    pl.semaphore_signal(barrier, 1, device_id=sibling)
    pl.semaphore_signal(barrier, 1, device_id=far)
    for distance in (-2, -1, 1, 2):
        for j in range(4):
            pl.semaphore_signal(barrier, 1, device_id=(group(distance), j))

    loads = [
        pltpu.make_async_copy(small_hbm, small, table_sem.at[0]),
        pltpu.make_async_copy(large_hbm, large, table_sem.at[1]),
        pltpu.make_async_copy(along_hbm.at[me], along_x, table_sem.at[2]),
        pltpu.make_async_copy(screened_hbm, screened, table_sem.at[3]),
    ]
    for load in loads:
        load.start()
    for k in range(18):
        lanes = pl.ds(128 * k, 128)
        for r in range(SLAB):
            spread_rows[k, pl.ds(r, GROUP, stride=SLAB), :] = arrived[r, :, lanes].astype(jnp.float32)
        home_in[0, :, lanes] = spread_rows[k].astype(jnp.bfloat16)
        for i in range(GROUP):
            orbitals[i, :, lanes] = spread_rows[k, pl.ds(SLAB * i, SLAB), :].astype(jnp.bfloat16)
    vis_sum[...] = jnp.zeros_like(vis_sum)
    pl.semaphore_wait(barrier, 18)

    def home_copy(source, slot, target):
        return pltpu.make_async_remote_copy(
            source, home_in.at[slot], home_send.at[slot], home_recv.at[slot], device_id=target
        )

    def xor(a, j):
        low = lax.rem(a + j, 2)
        high = lax.rem(a // 2 + j // 2, 2)
        return 2 * high + low

    far_copy = home_copy(home_in.at[0], 2, far)
    far_copy.start()
    sib_copy = home_copy(home_in.at[0], 1, sibling)
    sib_copy.start()
    vis_copies = []

    def send_visitors(s):
        for j in range(4):
            copy = pltpu.make_async_remote_copy(
                orbitals.at[j],
                vis_in.at[s, xor(me, j)],
                vis_send.at[s, j],
                vis_recv.at[s, xor(me, j)],
                device_id=(group(s + 1), j),
            )
            copy.start()
            vis_copies.append(copy)

    send_visitors(1)

    def widen(s, slots):
        for q in slots:
            pltpu.make_async_remote_copy(
                orbitals.at[0], vis_in.at[s, q], vis_send.at[s, 0], vis_recv.at[s, q],
                device_id=sibling,
            ).wait_recv()
            value = vis_in[s, q].astype(jnp.float32)
            for i in range(GROUP):
                wide[s, q, pl.ds(SLAB * i, SLAB), :] = value

    def forward(pairs):
        for cls in range(4):
            first, lanes = CLASSES[cls]
            value = plane(pairs, cls, (z_hi, z_lo), weights(small, large, 0, cls))
            for k, row in enumerate(segments(pairs)):
                at = (pl.ds(row, POINTS), pl.ds(first, lanes))
                s_hi[at], s_lo[at] = parted(value[POINTS * k : POINTS * k + POINTS])

    def backward(pairs):
        for cls in range(4):
            first, lanes = CLASSES[cls]
            value = plane(pairs, cls, (s_hi, s_lo), weights(small, large, 1, cls))
            for k, row in enumerate(segments(pairs)):
                g[pl.ds(row, POINTS), pl.ds(first, lanes)] = value[POINTS * k : POINTS * k + POINTS]

    def across():
        for start in range(0, PLANE, 768):
            middle(start, (s_hi, s_lo), (s_hi, s_lo), along_x, screened)

    sib_copy.wait_recv()
    widen(1, (0, 1))
    densities(0, home_in, wide.at[1], z_hi, z_lo)
    for load in loads:
        load.wait()
    forward((0,))
    far_copy.wait_recv()
    relay = home_copy(home_in.at[2], 3, sibling)
    relay.start()
    widen(1, (2, 3))
    send_visitors(0)
    relay.wait_recv()
    densities(1, home_in, wide.at[1], z_hi, z_lo)
    forward((1,))
    across()
    backward((0, 1))
    for q in range(4):
        products(q, False, home_in, wide.at[1], g, home_sum, vis_sum.at[1])

    def send_back(s, q):
        code_visitor(vis_sum.at[s, q], vis_code.at[s, q])
        copy = pltpu.make_async_remote_copy(
            vis_code.at[s, q],
            vis_back.at[s, me],
            back_send.at[s, q],
            back_recv.at[s, me],
            device_id=(group(-s - 1), xor(me, q)),
        )
        copy.start()
        return copy

    back_copies = [send_back(1, q) for q in range(4)]

    widen(0, range(4))
    densities(0, home_in, wide.at[0], z_hi, z_lo)
    densities(1, home_in, wide.at[0], z_hi, z_lo)
    forward((0, 1))
    across()

    def sum_copy(source, target_ref, slot, target):
        return pltpu.make_async_remote_copy(
            source, target_ref, sum_send.at[slot], sum_recv.at[slot], device_id=target
        )

    backward((1,))
    products(3, True, home_in, wide.at[0], g, home_sum, vis_sum.at[0])
    to_relay = sum_copy(home_sum.at[3], sib_relay, 0, sibling)
    to_relay.start()
    products(2, True, home_in, wide.at[0], g, home_sum, vis_sum.at[0])
    back_copies += [send_back(0, 3), send_back(0, 2)]
    to_relay.wait_recv()
    columns = [pl.ds(128 * k, 128) for k in range(18)]
    for lanes in columns:
        far_sum[:, lanes] = home_sum[2, :, lanes] + sib_relay[:, lanes]
    scale = scale_of([far_sum[:, lanes] for lanes in columns])
    for lanes in columns:
        far_out[:, lanes] = coded(far_sum[:, lanes], scale)
    far_out[:, pl.ds(PLANE, 128)] = jnp.broadcast_to(scale, (POINTS, 128)).astype(jnp.bfloat16)
    to_far = sum_copy(far_out, far_in, 1, far)
    to_far.start()
    backward((0,))
    products(1, True, home_in, wide.at[0], g, home_sum, vis_sum.at[0])
    to_final = sum_copy(home_sum.at[1], sib_final, 2, sibling)
    to_final.start()
    products(0, True, home_in, wide.at[0], g, home_sum, vis_sum.at[0])
    back_copies += [send_back(0, 1), send_back(0, 0)]

    to_final.wait_recv()
    for s in (1, 0):
        for j in range(4):
            pltpu.make_async_remote_copy(
                vis_code.at[s, 0], vis_back.at[s, j], back_send.at[s, 0], back_recv.at[s, j],
                device_id=sibling,
            ).wait_recv()
    to_far.wait_recv()
    far_inverse = 1.0 / far_in[pl.ds(0, 16), pl.ds(PLANE, 128)].astype(jnp.float32)[:1]
    vis_inverse = [
        [1.0 / vis_back[s, i, pl.ds(32, 16), pl.ds(384, 128)].astype(jnp.float32)[15:] for i in range(4)]
        for s in range(2)
    ]
    for k in range(18):
        lanes = pl.ds(128 * k, 128)
        total = home_sum[0, :, lanes] + sib_final[:, lanes] + decoded(far_in[:, lanes], far_inverse)
        part, place = divmod(k, 5)
        for i in range(GROUP):
            values = [
                decoded(vis_back[s, i, :, pl.ds(128 * place, 128)], vis_inverse[s][i])
                for s in range(2)
            ]
            back = values[0] + values[1]
            mine = total[SLAB * i : SLAB * i + SLAB] + back[SLAB * part : SLAB * part + SLAB]
            out[:, i, lanes] = mine

    for copy in [far_copy, sib_copy, relay, to_relay, to_far, to_final] + vis_copies + back_copies:
        copy.wait_send()


def solution(mesh):
    small, large, along_x, screened = tables()
    any_space = pl.BlockSpec(memory_space=pl.ANY)
    bf16, f32 = jnp.bfloat16, jnp.float32
    dma = pltpu.SemaphoreType.DMA
    call = pl.pallas_call(
        kernel,
        out_shape=jax.ShapeDtypeStruct((SLAB, GROUP, PLANE), f32),
        in_specs=[pl.BlockSpec(memory_space=pltpu.VMEM)] + [any_space] * 4,
        out_specs=pl.BlockSpec(memory_space=pltpu.VMEM),
        scratch_shapes=[
            pltpu.VMEM((18, POINTS, 128), f32),
            pltpu.VMEM((GROUP, SLAB, PLANE), bf16),
            pltpu.VMEM((4, POINTS, PLANE), bf16),
            pltpu.VMEM((2, 4, SLAB, PLANE), bf16),
            pltpu.VMEM((2, 4, POINTS, PLANE), f32),
            pltpu.VMEM((ROWS, PLANE), bf16),
            pltpu.VMEM((ROWS, PLANE), bf16),
            pltpu.VMEM((ROWS, PLANE), bf16),
            pltpu.VMEM((ROWS, PLANE), bf16),
            pltpu.VMEM((ROWS, PLANE), f32),
            pltpu.VMEM((4, POINTS, PLANE), f32),
            pltpu.VMEM((2, 4, POINTS, 640), f32),
            pltpu.VMEM((2, 4, POINTS, 640), bf16),
            pltpu.VMEM((POINTS, PLANE), f32),
            pltpu.VMEM((POINTS, PLANE), f32),
            pltpu.VMEM((POINTS, PLANE), f32),
            pltpu.VMEM((POINTS, PLANE + 128), bf16),
            pltpu.VMEM((POINTS, PLANE + 128), bf16),
            pltpu.VMEM((2, 4, POINTS, 640), bf16),
            pltpu.VMEM(small.shape, bf16),
            pltpu.VMEM(large.shape, bf16),
            pltpu.VMEM(along_x.shape[1:], bf16),
            pltpu.VMEM(screened.shape, f32),
            dma((4,)), dma((4,)), dma((4,)), dma((2, 4)), dma((2, 4)),
            dma((3,)), dma((3,)), dma((2, 4)), dma((2, 4)),
        ],
        compiler_params=pltpu.CompilerParams(
            collective_id=0, has_side_effects=True, vmem_limit_bytes=60 << 20
        ),
    )

    def body(orbitals):
        return -MIXING * jnp.transpose(
            call(jnp.transpose(orbitals, (1, 0, 2)), small, large, along_x, screened), (1, 0, 2)
        )

    placed = P("band", "grid", None)
    return jax.shard_map(
        body, mesh=mesh, in_specs=(placed,), out_specs=placed, check_vma=False
    )
```

```python
import functools

import jax
import jax.numpy as jnp
import ml_dtypes
import numpy as np
from jax import lax
from jax.experimental import pallas as pl
from jax.experimental.pallas import tpu as pltpu
from jax.sharding import PartitionSpec as P

POINTS = 48
PLANE = POINTS * POINTS
GROUP = 4
SLAB = 12
BAND = 64
CHUNK = 384
BOX = 37.25
OMEGA = 0.106
MIXING = 0.25
ROWS = 4 * GROUP * SLAB
HALF = ROWS // 2
BEHIND = (-1, 2)
CLASSES = ((0, 384), (384, 384), (768, 768), (1536, 768))


def halves(table):
    high = table.astype(ml_dtypes.bfloat16)
    low = (table - high.astype(np.float64)).astype(ml_dtypes.bfloat16)
    return high, low


def tables():
    index = np.arange(POINTS)
    angles = 2.0 * np.pi * (np.outer(index, index) % POINTS) / POINTS
    cas = np.cos(angles) + np.sin(angles)

    def spread(weights):
        rows = np.zeros((8, POINTS))
        for fine in range(8):
            rows[fine, fine::8] = weights
        return rows

    even, odd = [1, 1, 1, 1, 1, 1], [1, -1, 1, -1, 1, -1]
    real2, imag2 = [1, -0.5, -0.5, 1, -0.5, -0.5], [0, 1, -1, 0, 1, -1]
    real1, imag1 = [1, 0.5, -0.5, -1, -0.5, 0.5], [0, 1, 1, 0, -1, -1]
    matrices, order = [], []
    for parts, residues in (
        ((even,), (0,)),
        ((odd,), (3,)),
        ((real2, imag2), (2, 4)),
        ((real1, imag1), (1, 5)),
    ):
        folded = np.concatenate([spread(part) for part in parts])
        waves = [k for k in range(POINTS) if k % 6 in residues]
        small = cas[waves] @ folded.T @ np.linalg.inv(folded @ folded.T)
        matrices.append(np.kron(small, cas))
        order += waves
    signed = ((index + POINTS // 2) % POINTS - POINTS // 2) * (2.0 * np.pi / BOX)
    along_y, along_z = np.repeat(np.array(order), POINTS), np.tile(index, POINTS)
    squares = (
        signed[:, None] ** 2 + signed[along_y][None] ** 2 + signed[along_z][None] ** 2
    )
    bounded = np.where(squares > 0.0, squares, 1.0)
    screened = 4.0 * np.pi / bounded * (1.0 - np.exp(-bounded / (4.0 * OMEGA * OMEGA)))
    screened = np.where(squares > 0.0, screened, np.pi / (OMEGA * OMEGA)) / POINTS**3

    forward = [halves(m.T) for m in matrices]
    inverse = [halves(m) for m in matrices]
    small = np.stack([np.stack([w[c][p] for c in (0, 1) for p in (0, 1)]) for w in (forward, inverse)])
    large = np.stack([np.stack([w[c][p] for c in (2, 3) for p in (0, 1)]) for w in (forward, inverse)])

    along = []
    for device in range(4):
        matrix = np.zeros((2, POINTS, 4, 2, SLAB))
        for slot in range(4):
            base = SLAB * (device ^ slot)
            for orbital in range(2):
                matrix[orbital, :, slot, orbital, :] = cas[:, base : base + SLAB]
        matrix = matrix.reshape(HALF, HALF)
        for source in (matrix, matrix.T):
            high, low = halves(source)
            top = np.concatenate([high, high], axis=1)
            bottom = np.concatenate([low, np.zeros_like(low)], axis=1)
            along.append(np.concatenate([top, bottom], axis=0))
    along_x = np.stack(along).reshape(4, 2, ROWS, ROWS)
    return small, large, along_x, screened.astype(np.float32)


def parted(value):
    high = value.astype(jnp.bfloat16)
    return high, (value - high.astype(jnp.float32)).astype(jnp.bfloat16)


def dot(left, right):
    return jnp.dot(left, right, preferred_element_type=jnp.float32)


def fold(d):
    s = [d[p] + d[p + 3] for p in range(3)]
    t = [d[p] - d[p + 3] for p in range(3)]
    u, v = s[1] + s[2], t[1] - t[2]
    return (s[0] + u, t[0] - v, s[0] - 0.5 * u, s[1] - s[2], t[0] + 0.5 * v, t[1] + t[2])


def unfold(f):
    z0, z3, r2, i2, r1, i1 = f
    a, b = z0 - 0.5 * r2, z3 - 0.5 * r1
    s = (z0 + r2, a + i2, a - i2)
    t = (z3 + r1, i1 - b, i1 + b)
    return [s[p] + t[p] for p in range(3)] + [s[p] - t[p] for p in range(3)]


def densities(pair, two, home_in, wide, z_hi, z_lo):
    for tile in range(3):
        d = [None] * 6
        for p in range(3):
            lanes = pl.ds(p * CHUNK + tile * 128, 128)
            values = [
                home_in[2 * pair + k, two, :, lanes].astype(jnp.float32) * wide[2 * pair + k, :, lanes]
                for k in range(2)
            ]
            d[p] = jnp.concatenate([value[:24] for value in values], axis=0)
            d[p + 3] = jnp.concatenate([value[24:] for value in values], axis=0)
        for p, value in enumerate(fold(d)):
            at = (pl.ds(HALF * two + POINTS * pair, POINTS), pl.ds(p * CHUNK + tile * 128, 128))
            z_hi[at], z_lo[at] = parted(value)


def weights(small, large, which, cls):
    return (small, large)[cls // 2], which, 2 * (cls % 2)


def plane(two, cls, source, table):
    ref, which, base = table
    first, lanes = CLASSES[cls]
    high, low = (part[pl.ds(HALF * two, HALF), pl.ds(first, lanes)] for part in source)
    both = dot(jnp.concatenate([high, low], axis=0), ref[which, base])
    return both[:HALF] + both[HALF:] + dot(high, ref[which, base + 1])


def middle(start, two, s, u, along_x, screened):
    at = (pl.ds(HALF * two, HALF), pl.ds(start, 768))
    table = screened[:, pl.ds(start, 768)]
    both = dot(along_x[0], jnp.concatenate([s[0][at], s[1][at]], axis=0))
    weighted = (both[:HALF] + both[HALF:]) * jnp.concatenate([table] * 2, axis=0)
    both = dot(along_x[1], jnp.concatenate(parted(weighted), axis=0))
    u[0][at], u[1][at] = parted(both[:HALF] + both[HALF:])


def products(q, two, last, home_in, wide, g, home_sum, vis_part, vis_sum):
    for tile in range(3):
        f = [g[pl.ds(HALF * two + 24 * q, 24), pl.ds(p * CHUNK + tile * 128, 128)] for p in range(6)]
        values = unfold(f)
        for p in range(3):
            lanes = pl.ds(p * CHUNK + tile * 128, 128)
            value = jnp.concatenate([values[p], values[p + 3]], axis=0)
            home = value * wide[q, :, lanes]
            if last:
                home = home + home_sum[q, two, :, lanes]
            home_sum[q, two, :, lanes] = home
            other = value * home_in[q, two, :, lanes].astype(jnp.float32)
            if two == 0:
                vis_part[q, :, lanes] = other
                continue
            other = other + vis_part[q, :, lanes]
            for half in range(2):
                rows = other[24 * half : 24 * half + SLAB] + other[24 * half + SLAB : 24 * half + 24]
                part, place = divmod(9 * half + 3 * p + tile, 5)
                vis_sum[q, pl.ds(SLAB * part, SLAB), pl.ds(128 * place, 128)] = rows


def scale_of(values):
    top = functools.reduce(jnp.maximum, [jnp.max(jnp.abs(v), axis=0, keepdims=True) for v in values])
    top = jnp.max(top, axis=1, keepdims=True)
    return (220.0 / jnp.maximum(top, 1e-30)).astype(jnp.bfloat16).astype(jnp.float32)


def coded(value, scale):
    power = value * scale
    for _ in range(4):
        power = power * power
    return jnp.where(value < 0.0, -power, power).astype(jnp.bfloat16)


def decoded(code, inverse):
    power = code.astype(jnp.float32)
    value = jnp.exp2(jnp.log2(jnp.abs(power)) * 0.0625) * inverse
    return jnp.where(power < 0.0, -value, value)


def code_visitor(source, target):
    tiles = [source[:, pl.ds(128 * k, 128)] for k in range(5)]
    scale = scale_of(tiles)
    spare = lax.broadcasted_iota(jnp.int32, (POINTS, 128), 0) >= 3 * SLAB
    for k in range(5):
        code = coded(tiles[k], scale)
        if k >= 3:
            code = jnp.where(spare, jnp.broadcast_to(scale, (POINTS, 128)), code.astype(jnp.float32))
        target[:, pl.ds(128 * k, 128)] = code.astype(jnp.bfloat16)


def kernel(
    arrived, small_hbm, large_hbm, along_hbm, screened_hbm, out,
    spread_rows, spread_parts, orbitals, home_in, vis_in, wide, z_hi, z_lo, s_hi, s_lo, g,
    home_sum, vis_part, vis_sum, vis_code, sib_relay, sib_final, far_sum, far_out, far_in, vis_back,
    small, large, along_x, screened,
    table_sem, home_send, home_recv, vis_send, vis_recv,
    sum_send, sum_recv, back_send, back_recv,
):
    band, me = lax.axis_index("band"), lax.axis_index("grid")

    def partner(bit):
        return me + bit - 2 * bit * (lax.rem(me // bit, 2))

    def group(distance):
        return lax.rem(band + distance + BAND, BAND)

    def xor(a, j):
        low = lax.rem(a + j, 2)
        high = lax.rem(a // 2 + j // 2, 2)
        return 2 * high + low

    sibling, far = (band, partner(1)), (band, partner(2))

    barrier = pltpu.get_barrier_semaphore()
    pl.semaphore_signal(barrier, 1, device_id=sibling)
    pl.semaphore_signal(barrier, 1, device_id=far)
    for distance in BEHIND:
        for j in range(4):
            pl.semaphore_signal(barrier, 1, device_id=(group(-distance), j))

    loads = [
        pltpu.make_async_copy(small_hbm, small, table_sem.at[0]),
        pltpu.make_async_copy(large_hbm, large, table_sem.at[1]),
        pltpu.make_async_copy(along_hbm.at[me], along_x, table_sem.at[2]),
        pltpu.make_async_copy(screened_hbm, screened, table_sem.at[3]),
    ]
    spread_parts[3:5] = jnp.zeros((2, ROWS, 128), jnp.float32)
    for k in range(18):
        part, place = divmod(k, 5)
        for r in range(SLAB):
            value = arrived[r, :, pl.ds(128 * k, 128)].astype(jnp.float32)
            spread_rows[k, pl.ds(r, GROUP, stride=SLAB), :] = value
            spread_parts[place, pl.ds(SLAB * part + r, GROUP, stride=POINTS), :] = value
    for i in range(GROUP):
        for place in range(5):
            orbitals[i, :, pl.ds(128 * place, 128)] = spread_parts[
                place, pl.ds(POINTS * i, POINTS), :
            ].astype(jnp.bfloat16)
    for two in range(2):
        for k in range(9):
            value = jnp.concatenate(
                [spread_rows[k + 9 * half, pl.ds(24 * two, 24), :] for half in range(2)], axis=0
            )
            home_in[0, two, :, pl.ds(128 * k, 128)] = value.astype(jnp.bfloat16)
    vis_sum[:, :, pl.ds(32, 16), pl.ds(384, 256)] = jnp.zeros((2, 4, 16, 256), jnp.float32)
    pl.semaphore_wait(barrier, 10)

    def home_copy(source, slot, two, target):
        copy = pltpu.make_async_remote_copy(
            home_in.at[source, two],
            home_in.at[slot, two],
            home_send.at[slot, two],
            home_recv.at[slot, two],
            device_id=target,
        )
        copy.start()
        return copy

    sent = []

    def send_visitors(s):
        for j in range(4):
            copy = pltpu.make_async_remote_copy(
                orbitals.at[j],
                vis_in.at[s, xor(me, j)],
                vis_send.at[s, j],
                vis_recv.at[s, xor(me, j)],
                device_id=(group(BEHIND[s]), j),
            )
            copy.start()
            sent.append(copy)

    sib_copies = [home_copy(0, 1, 0, sibling)]
    send_visitors(0)
    far_copies = [home_copy(0, 2, 0, far)]
    sib_copies.append(home_copy(0, 1, 1, sibling))
    far_copies.append(home_copy(0, 2, 1, far))
    send_visitors(1)

    for load in loads:
        load.start()

    def widen(s, slots):
        for q in slots:
            pltpu.make_async_remote_copy(
                orbitals.at[0], vis_in.at[s, q], vis_send.at[s, 0], vis_recv.at[s, q],
                device_id=sibling,
            ).wait_recv()
            for place in range(5):
                value = vis_in[s, q, :, pl.ds(128 * place, 128)].astype(jnp.float32)
                for part in range(4 if place < 3 else 3):
                    half, k = divmod(5 * part + place, 9)
                    rows = value[SLAB * part : SLAB * part + SLAB]
                    for copy in range(2):
                        wide[s, q, pl.ds(24 * half + SLAB * copy, SLAB), pl.ds(128 * k, 128)] = rows

    def forward(two):
        for cls in range(4):
            first, lanes = CLASSES[cls]
            at = (pl.ds(HALF * two, HALF), pl.ds(first, lanes))
            value = plane(two, cls, (z_hi, z_lo), weights(small, large, 0, cls))
            s_hi[at], s_lo[at] = parted(value)

    def backward(two):
        for cls in range(4):
            first, lanes = CLASSES[cls]
            at = (pl.ds(HALF * two, HALF), pl.ds(first, lanes))
            g[at] = plane(two, cls, (s_hi, s_lo), weights(small, large, 1, cls))

    def across(two):
        for start in range(0, PLANE, 768):
            middle(start, two, (s_hi, s_lo), (s_hi, s_lo), along_x, screened)

    def slab(q, two, s):
        products(q, two, s == 1, home_in, wide.at[s], g, home_sum, vis_part, vis_sum.at[s])

    def send_back(s, q):
        code_visitor(vis_sum.at[s, q], vis_code.at[s, q])
        copy = pltpu.make_async_remote_copy(
            vis_code.at[s, q],
            vis_back.at[s, me],
            back_send.at[s, q],
            back_recv.at[s, me],
            device_id=(group(-BEHIND[s]), xor(me, q)),
        )
        copy.start()
        sent.append(copy)

    def sum_copy(source, target_ref, two, kind, target):
        copy = pltpu.make_async_remote_copy(
            source, target_ref, sum_send.at[two, kind], sum_recv.at[two, kind], device_id=target
        )
        copy.start()
        sent.append(copy)
        return copy

    columns = [pl.ds(128 * k, 128) for k in range(9)]

    def to_far(two, relayed):
        relayed.wait_recv()
        for lanes in columns:
            far_sum[:, lanes] = home_sum[2, two, :, lanes] + sib_relay[two, :, lanes]
        scale = scale_of([far_sum[:, lanes] for lanes in columns])
        for lanes in columns:
            far_out[two, :, lanes] = coded(far_sum[:, lanes], scale)
        far_out[two, :, pl.ds(PLANE // 2, 128)] = jnp.broadcast_to(scale, (POINTS, 128)).astype(jnp.bfloat16)
        return sum_copy(far_out.at[two], far_in.at[two], two, 1, far)

    sib_copies[0].wait_recv()
    widen(0, (0, 1))
    densities(0, 0, home_in, wide.at[0], z_hi, z_lo)
    far_copies[0].wait_recv()
    relays = [home_copy(2, 3, 0, sibling)]
    widen(0, (2, 3))
    relays[0].wait_recv()
    densities(1, 0, home_in, wide.at[0], z_hi, z_lo)
    for load in loads:
        load.wait()
    forward(0)
    across(0)
    backward(0)
    far_copies[1].wait_recv()
    relays.append(home_copy(2, 3, 1, sibling))
    for q in range(4):
        slab(q, 0, 0)

    sib_copies[1].wait_recv()
    densities(0, 1, home_in, wide.at[0], z_hi, z_lo)
    relays[1].wait_recv()
    densities(1, 1, home_in, wide.at[0], z_hi, z_lo)
    forward(1)
    across(1)
    backward(1)
    for q in (2, 3, 0, 1):
        slab(q, 1, 0)
        send_back(0, q)

    widen(1, range(4))
    for pair in range(2):
        densities(pair, 0, home_in, wide.at[1], z_hi, z_lo)
    forward(0)
    across(0)
    backward(0)
    slab(3, 0, 1)
    relayed = sum_copy(home_sum.at[3, 0], sib_relay.at[0], 0, 0, sibling)
    slab(2, 0, 1)
    slab(1, 0, 1)
    finals = [sum_copy(home_sum.at[1, 0], sib_final.at[0], 0, 2, sibling)]
    slab(0, 0, 1)

    for pair in range(2):
        densities(pair, 1, home_in, wide.at[1], z_hi, z_lo)
    fars = [to_far(0, relayed)]
    forward(1)
    across(1)
    backward(1)
    slab(3, 1, 1)
    relayed = sum_copy(home_sum.at[3, 1], sib_relay.at[1], 1, 0, sibling)
    send_back(1, 3)
    slab(2, 1, 1)
    send_back(1, 2)
    fars.append(to_far(1, relayed))
    slab(1, 1, 1)
    finals.append(sum_copy(home_sum.at[1, 1], sib_final.at[1], 1, 2, sibling))
    slab(0, 1, 1)
    send_back(1, 1)
    send_back(1, 0)

    def returned(s):
        for j in range(4):
            pltpu.make_async_remote_copy(
                vis_code.at[s, 0], vis_back.at[s, j], back_send.at[s, 0], back_recv.at[s, j],
                device_id=sibling,
            ).wait_recv()
        return [
            1.0 / vis_back[s, i, pl.ds(32, 16), pl.ds(384, 128)].astype(jnp.float32)[15:] for i in range(4)
        ]

    def far_scale(two):
        return 1.0 / far_in[two, pl.ds(0, 16), pl.ds(PLANE // 2, 128)].astype(jnp.float32)[:1]

    finals[0].wait_recv()
    fars[0].wait_recv()
    inverse = far_scale(0)
    for lanes in columns:
        home_sum[0, 0, :, lanes] = (
            home_sum[0, 0, :, lanes] + sib_final[0, :, lanes] + decoded(far_in[0, :, lanes], inverse)
        )
    inverses = returned(0)
    for i in range(GROUP):
        for place in range(5):
            lanes = pl.ds(128 * place, 128)
            vis_sum[1, i, :, lanes] = decoded(vis_back[0, i, :, lanes], inverses[i])
    finals[1].wait_recv()
    for lanes in columns:
        home_sum[0, 1, :, lanes] = home_sum[0, 1, :, lanes] + sib_final[1, :, lanes]
    inverses = returned(1)
    for i in range(GROUP):
        for place in range(5):
            lanes = pl.ds(128 * place, 128)
            vis_sum[1, i, :, lanes] = vis_sum[1, i, :, lanes] + decoded(vis_back[1, i, :, lanes], inverses[i])
    fars[1].wait_recv()
    inverse = far_scale(1)
    for k in range(9):
        lanes = pl.ds(128 * k, 128)
        totals = [
            home_sum[0, 0, :, lanes],
            home_sum[0, 1, :, lanes] + decoded(far_in[1, :, lanes], inverse),
        ]
        for half in range(2):
            column = k + 9 * half
            part, place = divmod(column, 5)
            for i in range(GROUP):
                row = 24 * half + SLAB * (i % 2)
                back = vis_sum[1, i, pl.ds(SLAB * part, SLAB), pl.ds(128 * place, 128)]
                out[:, i, pl.ds(128 * column, 128)] = totals[i // 2][row : row + SLAB] + back

    for copy in far_copies + sib_copies + relays + sent:
        copy.wait_send()


def solution(mesh):
    small, large, along_x, screened = tables()
    any_space = pl.BlockSpec(memory_space=pl.ANY)
    bf16, f32 = jnp.bfloat16, jnp.float32
    dma = pltpu.SemaphoreType.DMA
    call = pl.pallas_call(
        kernel,
        out_shape=pltpu.VMEM((SLAB, GROUP, PLANE), f32),
        in_specs=[pl.BlockSpec(memory_space=pltpu.VMEM)] + [any_space] * 4,
        out_specs=pl.BlockSpec(memory_space=pltpu.VMEM),
        scratch_shapes=[
            pltpu.VMEM((18, POINTS, 128), f32),
            pltpu.VMEM((5, ROWS, 128), f32),
            pltpu.VMEM((GROUP, POINTS, 640), bf16),
            pltpu.VMEM((4, 2, POINTS, PLANE // 2), bf16),
            pltpu.VMEM((2, 4, POINTS, 640), bf16),
            pltpu.VMEM((2, 4, POINTS, PLANE // 2), f32),
            pltpu.VMEM((ROWS, PLANE), bf16),
            pltpu.VMEM((ROWS, PLANE), bf16),
            pltpu.VMEM((ROWS, PLANE), bf16),
            pltpu.VMEM((ROWS, PLANE), bf16),
            pltpu.VMEM((ROWS, PLANE), f32),
            pltpu.VMEM((4, 2, POINTS, PLANE // 2), f32),
            pltpu.VMEM((4, POINTS, PLANE // 2), f32),
            pltpu.VMEM((2, 4, POINTS, 640), f32),
            pltpu.VMEM((2, 4, POINTS, 640), bf16),
            pltpu.VMEM((2, POINTS, PLANE // 2), f32),
            pltpu.VMEM((2, POINTS, PLANE // 2), f32),
            pltpu.VMEM((POINTS, PLANE // 2), f32),
            pltpu.VMEM((2, POINTS, PLANE // 2 + 128), bf16),
            pltpu.VMEM((2, POINTS, PLANE // 2 + 128), bf16),
            pltpu.VMEM((2, 4, POINTS, 640), bf16),
            pltpu.VMEM(small.shape, bf16),
            pltpu.VMEM(large.shape, bf16),
            pltpu.VMEM(along_x.shape[1:], bf16),
            pltpu.VMEM(screened.shape, f32),
            dma((4,)), dma((4, 2)), dma((4, 2)), dma((2, 4)), dma((2, 4)),
            dma((2, 3)), dma((2, 3)), dma((2, 4)), dma((2, 4)),
        ],
        compiler_params=pltpu.CompilerParams(
            collective_id=0, has_side_effects=True, vmem_limit_bytes=60 << 20
        ),
    )

    def body(orbitals):
        return -MIXING * jnp.transpose(
            call(jnp.transpose(orbitals, (1, 0, 2)), small, large, along_x, screened), (1, 0, 2)
        )

    placed = P("band", "grid", None)
    return jax.shard_map(
        body, mesh=mesh, in_specs=(placed,), out_specs=placed, check_vma=False
    )
```

```python
import functools

import jax
import jax.numpy as jnp
import ml_dtypes
import numpy as np
from jax import lax
from jax.experimental import pallas as pl
from jax.experimental.pallas import tpu as pltpu
from jax.sharding import PartitionSpec as P

POINTS = 48
PLANE = POINTS * POINTS
GROUP = 4
SLAB = 12
BAND = 64
CHUNK = 384
BOX = 37.25
OMEGA = 0.106
MIXING = 0.25
ROWS = 4 * GROUP * SLAB
HALF = ROWS // 2
BEHIND = (-1, 2)
CLASSES = ((0, 384), (384, 384), (768, 768), (1536, 768))


def halves(table):
    high = table.astype(ml_dtypes.bfloat16)
    low = (table - high.astype(np.float64)).astype(ml_dtypes.bfloat16)
    return high, low


def tables():
    index = np.arange(POINTS)
    angles = 2.0 * np.pi * (np.outer(index, index) % POINTS) / POINTS
    cas = np.cos(angles) + np.sin(angles)

    def spread(weights):
        rows = np.zeros((8, POINTS))
        for fine in range(8):
            rows[fine, fine::8] = weights
        return rows

    even, odd = [1, 1, 1, 1, 1, 1], [1, -1, 1, -1, 1, -1]
    real2, imag2 = [1, -0.5, -0.5, 1, -0.5, -0.5], [0, 1, -1, 0, 1, -1]
    real1, imag1 = [1, 0.5, -0.5, -1, -0.5, 0.5], [0, 1, 1, 0, -1, -1]
    matrices, order = [], []
    for parts, residues in (
        ((even,), (0,)),
        ((odd,), (3,)),
        ((real2, imag2), (2, 4)),
        ((real1, imag1), (1, 5)),
    ):
        folded = np.concatenate([spread(part) for part in parts])
        waves = [k for k in range(POINTS) if k % 6 in residues]
        small = cas[waves] @ folded.T @ np.linalg.inv(folded @ folded.T)
        matrices.append(np.kron(small, cas))
        order += waves
    signed = ((index + POINTS // 2) % POINTS - POINTS // 2) * (2.0 * np.pi / BOX)
    along_y, along_z = np.repeat(np.array(order), POINTS), np.tile(index, POINTS)
    squares = (
        signed[:, None] ** 2 + signed[along_y][None] ** 2 + signed[along_z][None] ** 2
    )
    bounded = np.where(squares > 0.0, squares, 1.0)
    screened = 4.0 * np.pi / bounded * (1.0 - np.exp(-bounded / (4.0 * OMEGA * OMEGA)))
    screened = np.where(squares > 0.0, screened, np.pi / (OMEGA * OMEGA)) / POINTS**3

    forward = [halves(m.T) for m in matrices]
    inverse = [halves(m) for m in matrices]
    small = np.stack([np.stack([w[c][p] for c in (0, 1) for p in (0, 1)]) for w in (forward, inverse)])
    large = np.stack([np.stack([w[c][p] for c in (2, 3) for p in (0, 1)]) for w in (forward, inverse)])

    along = []
    for device in range(4):
        matrix = np.zeros((2, POINTS, 4, 2, SLAB))
        for slot in range(4):
            base = SLAB * (device ^ slot)
            for orbital in range(2):
                matrix[orbital, :, slot, orbital, :] = cas[:, base : base + SLAB]
        matrix = matrix.reshape(HALF, HALF)
        for source in (matrix, matrix.T):
            high, low = halves(source)
            top = np.concatenate([high, high], axis=1)
            bottom = np.concatenate([low, np.zeros_like(low)], axis=1)
            along.append(np.concatenate([top, bottom], axis=0))
    along_x = np.stack(along).reshape(4, 2, ROWS, ROWS)
    return small, large, along_x, screened.astype(np.float32)


def parted(value):
    high = value.astype(jnp.bfloat16)
    return high, (value - high.astype(jnp.float32)).astype(jnp.bfloat16)


def dot(left, right):
    return jnp.dot(left, right, preferred_element_type=jnp.float32)


def fold(d):
    s = [d[p] + d[p + 3] for p in range(3)]
    t = [d[p] - d[p + 3] for p in range(3)]
    u, v = s[1] + s[2], t[1] - t[2]
    return (s[0] + u, t[0] - v, s[0] - 0.5 * u, s[1] - s[2], t[0] + 0.5 * v, t[1] + t[2])


def unfold(f):
    z0, z3, r2, i2, r1, i1 = f
    a, b = z0 - 0.5 * r2, z3 - 0.5 * r1
    s = (z0 + r2, a + i2, a - i2)
    t = (z3 + r1, i1 - b, i1 + b)
    return [s[p] + t[p] for p in range(3)] + [s[p] - t[p] for p in range(3)]


def densities(pair, two, home_in, wide, z_hi, z_lo):
    for tile in range(3):
        d = [None] * 6
        for p in range(3):
            lanes = pl.ds(p * CHUNK + tile * 128, 128)
            values = [
                home_in[2 * pair + k, two, :, lanes].astype(jnp.float32) * wide[2 * pair + k, :, lanes]
                for k in range(2)
            ]
            d[p] = jnp.concatenate([value[:24] for value in values], axis=0)
            d[p + 3] = jnp.concatenate([value[24:] for value in values], axis=0)
        for p, value in enumerate(fold(d)):
            at = (pl.ds(HALF * two + POINTS * pair, POINTS), pl.ds(p * CHUNK + tile * 128, 128))
            z_hi[at], z_lo[at] = parted(value)


def weights(small, large, which, cls):
    return (small, large)[cls // 2], which, 2 * (cls % 2)


def plane(two, cls, source, table):
    ref, which, base = table
    first, lanes = CLASSES[cls]
    high, low = (part[pl.ds(HALF * two, HALF), pl.ds(first, lanes)] for part in source)
    both = dot(jnp.concatenate([high, low], axis=0), ref[which, base])
    return both[:HALF] + both[HALF:] + dot(high, ref[which, base + 1])


def middle(start, two, s, u, along_x, screened):
    at = (pl.ds(HALF * two, HALF), pl.ds(start, 768))
    table = screened[:, pl.ds(start, 768)]
    both = dot(along_x[0], jnp.concatenate([s[0][at], s[1][at]], axis=0))
    weighted = (both[:HALF] + both[HALF:]) * jnp.concatenate([table] * 2, axis=0)
    both = dot(along_x[1], jnp.concatenate(parted(weighted), axis=0))
    u[0][at], u[1][at] = parted(both[:HALF] + both[HALF:])


def products(q, two, last, home_in, wide, g, home_sum, vis_part, vis_sum):
    for tile in range(3):
        f = [g[pl.ds(HALF * two + 24 * q, 24), pl.ds(p * CHUNK + tile * 128, 128)] for p in range(6)]
        values = unfold(f)
        for p in range(3):
            lanes = pl.ds(p * CHUNK + tile * 128, 128)
            value = jnp.concatenate([values[p], values[p + 3]], axis=0)
            home = value * wide[q, :, lanes]
            if last:
                home = home + home_sum[q, two, :, lanes]
            home_sum[q, two, :, lanes] = home
            other = value * home_in[q, two, :, lanes].astype(jnp.float32)
            if two == 0:
                vis_part[q, :, lanes] = other
                continue
            other = other + vis_part[q, :, lanes]
            for half in range(2):
                rows = other[24 * half : 24 * half + SLAB] + other[24 * half + SLAB : 24 * half + 24]
                part, place = divmod(9 * half + 3 * p + tile, 5)
                vis_sum[q, pl.ds(SLAB * part, SLAB), pl.ds(128 * place, 128)] = rows


def scale_of(values):
    top = functools.reduce(jnp.maximum, [jnp.max(jnp.abs(v), axis=0, keepdims=True) for v in values])
    top = jnp.max(top, axis=1, keepdims=True)
    return (220.0 / jnp.maximum(top, 1e-30)).astype(jnp.bfloat16).astype(jnp.float32)


def coded(value, scale):
    power = value * scale
    for _ in range(4):
        power = power * power
    return jnp.where(value < 0.0, -power, power).astype(jnp.bfloat16)


def decoded(code, inverse):
    power = code.astype(jnp.float32)
    value = jnp.exp2(jnp.log2(jnp.abs(power)) * 0.0625) * inverse
    return jnp.where(power < 0.0, -value, value)


def code_visitor(source, target):
    tiles = [source[:, pl.ds(128 * k, 128)] for k in range(5)]
    scale = scale_of(tiles)
    spare = lax.broadcasted_iota(jnp.int32, (POINTS, 128), 0) >= 3 * SLAB
    for k in range(5):
        code = coded(tiles[k], scale)
        if k >= 3:
            code = jnp.where(spare, jnp.broadcast_to(scale, (POINTS, 128)), code.astype(jnp.float32))
        target[:, pl.ds(128 * k, 128)] = code.astype(jnp.bfloat16)


def kernel(
    arrived, small_hbm, large_hbm, along_hbm, screened_hbm, out,
    spread_rows, spread_parts, orbitals, home_in, vis_in, wide, z_hi, z_lo, s_hi, s_lo, g,
    home_sum, vis_part, vis_sum, vis_code, sib_relay, sib_final, far_sum, far_out, far_in, vis_back,
    small, large, along_x, screened,
    table_sem, home_send, home_recv, vis_send, vis_recv,
    sum_send, sum_recv, back_send, back_recv,
):
    band, me = lax.axis_index("band"), lax.axis_index("grid")

    def partner(bit):
        return me + bit - 2 * bit * (lax.rem(me // bit, 2))

    def group(distance):
        return lax.rem(band + distance + BAND, BAND)

    def xor(a, j):
        low = lax.rem(a + j, 2)
        high = lax.rem(a // 2 + j // 2, 2)
        return 2 * high + low

    sibling, far = (band, partner(1)), (band, partner(2))

    barrier = pltpu.get_barrier_semaphore()
    pl.semaphore_signal(barrier, 1, device_id=sibling)
    pl.semaphore_signal(barrier, 1, device_id=far)
    for distance in BEHIND:
        for j in range(4):
            pl.semaphore_signal(barrier, 1, device_id=(group(-distance), j))

    loads = [
        pltpu.make_async_copy(small_hbm, small, table_sem.at[0]),
        pltpu.make_async_copy(large_hbm, large, table_sem.at[1]),
        pltpu.make_async_copy(along_hbm.at[me], along_x, table_sem.at[2]),
        pltpu.make_async_copy(screened_hbm, screened, table_sem.at[3]),
    ]
    spread_parts[3:5] = jnp.zeros((2, ROWS, 128), jnp.float32)
    for k in range(18):
        part, place = divmod(k, 5)
        for r in range(SLAB):
            value = arrived[r, :, pl.ds(128 * k, 128)].astype(jnp.float32)
            spread_rows[k, pl.ds(r, GROUP, stride=SLAB), :] = value
            spread_parts[place, pl.ds(SLAB * part + r, GROUP, stride=POINTS), :] = value
    for i in range(GROUP):
        for place in range(5):
            orbitals[i, :, pl.ds(128 * place, 128)] = spread_parts[
                place, pl.ds(POINTS * i, POINTS), :
            ].astype(jnp.bfloat16)
    for two in range(2):
        for k in range(9):
            value = jnp.concatenate(
                [spread_rows[k + 9 * half, pl.ds(24 * two, 24), :] for half in range(2)], axis=0
            )
            home_in[0, two, :, pl.ds(128 * k, 128)] = value.astype(jnp.bfloat16)
    vis_sum[:, :, pl.ds(32, 16), pl.ds(384, 256)] = jnp.zeros((2, 4, 16, 256), jnp.float32)
    pl.semaphore_wait(barrier, 10)

    def home_copy(source, slot, two, target):
        copy = pltpu.make_async_remote_copy(
            home_in.at[source, two],
            home_in.at[slot, two],
            home_send.at[slot, two],
            home_recv.at[slot, two],
            device_id=target,
        )
        copy.start()
        return copy

    visits = [
        [
            pltpu.make_async_remote_copy(
                orbitals.at[j],
                vis_in.at[s, xor(me, j)],
                vis_send.at[s, j],
                vis_recv.at[s, xor(me, j)],
                device_id=(group(BEHIND[s]), j),
            )
            for j in range(4)
        ]
        for s in range(2)
    ]
    sent = visits[0] + visits[1]

    def send_visitors(s):
        for copy in visits[s]:
            copy.start()

    turn = lax.rem(band // 2, 8) == 7
    sib_copies = [home_copy(0, 1, 0, sibling)]
    send_visitors(0)
    pl.when(turn)(functools.partial(send_visitors, 1))
    far_copies = [home_copy(0, 2, 0, far)]
    sib_copies.append(home_copy(0, 1, 1, sibling))
    far_copies.append(home_copy(0, 2, 1, far))

    for load in loads:
        load.start()

    def widen(s, slots):
        for q in slots:
            pltpu.make_async_remote_copy(
                orbitals.at[0], vis_in.at[s, q], vis_send.at[s, 0], vis_recv.at[s, q],
                device_id=sibling,
            ).wait_recv()
            for place in range(5):
                value = vis_in[s, q, :, pl.ds(128 * place, 128)].astype(jnp.float32)
                for part in range(4 if place < 3 else 3):
                    half, k = divmod(5 * part + place, 9)
                    rows = value[SLAB * part : SLAB * part + SLAB]
                    for copy in range(2):
                        wide[s, q, pl.ds(24 * half + SLAB * copy, SLAB), pl.ds(128 * k, 128)] = rows

    def forward(two):
        for cls in range(4):
            first, lanes = CLASSES[cls]
            at = (pl.ds(HALF * two, HALF), pl.ds(first, lanes))
            value = plane(two, cls, (z_hi, z_lo), weights(small, large, 0, cls))
            s_hi[at], s_lo[at] = parted(value)

    def backward(two):
        for cls in range(4):
            first, lanes = CLASSES[cls]
            at = (pl.ds(HALF * two, HALF), pl.ds(first, lanes))
            g[at] = plane(two, cls, (s_hi, s_lo), weights(small, large, 1, cls))

    def across(two):
        for start in range(0, PLANE, 768):
            middle(start, two, (s_hi, s_lo), (s_hi, s_lo), along_x, screened)

    def slab(q, two, s):
        products(q, two, s == 1, home_in, wide.at[s], g, home_sum, vis_part, vis_sum.at[s])

    def send_back(s, q):
        code_visitor(vis_sum.at[s, q], vis_code.at[s, q])
        copy = pltpu.make_async_remote_copy(
            vis_code.at[s, q],
            vis_back.at[s, me],
            back_send.at[s, q],
            back_recv.at[s, me],
            device_id=(group(-BEHIND[s]), xor(me, q)),
        )
        copy.start()
        sent.append(copy)

    def sum_copy(source, target_ref, two, kind, target):
        copy = pltpu.make_async_remote_copy(
            source, target_ref, sum_send.at[two, kind], sum_recv.at[two, kind], device_id=target
        )
        copy.start()
        sent.append(copy)
        return copy

    columns = [pl.ds(128 * k, 128) for k in range(9)]

    def to_far(two, relayed):
        relayed.wait_recv()
        for lanes in columns:
            far_sum[:, lanes] = home_sum[2, two, :, lanes] + sib_relay[two, :, lanes]
        scale = scale_of([far_sum[:, lanes] for lanes in columns])
        for lanes in columns:
            far_out[two, :, lanes] = coded(far_sum[:, lanes], scale)
        far_out[two, :, pl.ds(PLANE // 2, 128)] = jnp.broadcast_to(scale, (POINTS, 128)).astype(jnp.bfloat16)
        return sum_copy(far_out.at[two], far_in.at[two], two, 1, far)

    sib_copies[0].wait_recv()
    widen(0, (0, 1))
    densities(0, 0, home_in, wide.at[0], z_hi, z_lo)
    far_copies[0].wait_recv()
    relays = [home_copy(2, 3, 0, sibling)]
    pl.when(jnp.logical_not(turn))(functools.partial(send_visitors, 1))
    widen(0, (2, 3))
    relays[0].wait_recv()
    densities(1, 0, home_in, wide.at[0], z_hi, z_lo)
    for load in loads:
        load.wait()
    forward(0)
    across(0)
    backward(0)
    far_copies[1].wait_recv()
    relays.append(home_copy(2, 3, 1, sibling))
    for q in range(4):
        slab(q, 0, 0)

    sib_copies[1].wait_recv()
    densities(0, 1, home_in, wide.at[0], z_hi, z_lo)
    relays[1].wait_recv()
    densities(1, 1, home_in, wide.at[0], z_hi, z_lo)
    forward(1)
    across(1)
    backward(1)
    for q in (2, 3, 0, 1):
        slab(q, 1, 0)
        send_back(0, q)

    widen(1, range(4))
    for pair in range(2):
        densities(pair, 0, home_in, wide.at[1], z_hi, z_lo)
    forward(0)
    across(0)
    backward(0)
    slab(3, 0, 1)
    relayed = sum_copy(home_sum.at[3, 0], sib_relay.at[0], 0, 0, sibling)
    slab(2, 0, 1)
    slab(1, 0, 1)
    finals = [sum_copy(home_sum.at[1, 0], sib_final.at[0], 0, 2, sibling)]
    slab(0, 0, 1)

    for pair in range(2):
        densities(pair, 1, home_in, wide.at[1], z_hi, z_lo)
    fars = [to_far(0, relayed)]
    forward(1)
    across(1)
    backward(1)
    slab(3, 1, 1)
    relayed = sum_copy(home_sum.at[3, 1], sib_relay.at[1], 1, 0, sibling)
    send_back(1, 3)
    slab(2, 1, 1)
    send_back(1, 2)
    fars.append(to_far(1, relayed))
    slab(1, 1, 1)
    finals.append(sum_copy(home_sum.at[1, 1], sib_final.at[1], 1, 2, sibling))
    slab(0, 1, 1)
    send_back(1, 1)
    send_back(1, 0)

    def returned(s):
        for j in range(4):
            pltpu.make_async_remote_copy(
                vis_code.at[s, 0], vis_back.at[s, j], back_send.at[s, 0], back_recv.at[s, j],
                device_id=sibling,
            ).wait_recv()
        return [
            1.0 / vis_back[s, i, pl.ds(32, 16), pl.ds(384, 128)].astype(jnp.float32)[15:] for i in range(4)
        ]

    def far_scale(two):
        return 1.0 / far_in[two, pl.ds(0, 16), pl.ds(PLANE // 2, 128)].astype(jnp.float32)[:1]

    finals[0].wait_recv()
    fars[0].wait_recv()
    inverse = far_scale(0)
    for lanes in columns:
        home_sum[0, 0, :, lanes] = (
            home_sum[0, 0, :, lanes] + sib_final[0, :, lanes] + decoded(far_in[0, :, lanes], inverse)
        )
    inverses = returned(0)
    for i in range(GROUP):
        for place in range(5):
            lanes = pl.ds(128 * place, 128)
            vis_sum[1, i, :, lanes] = decoded(vis_back[0, i, :, lanes], inverses[i])
    finals[1].wait_recv()
    for lanes in columns:
        home_sum[0, 1, :, lanes] = home_sum[0, 1, :, lanes] + sib_final[1, :, lanes]
    inverses = returned(1)
    for i in range(GROUP):
        for place in range(5):
            lanes = pl.ds(128 * place, 128)
            vis_sum[1, i, :, lanes] = vis_sum[1, i, :, lanes] + decoded(vis_back[1, i, :, lanes], inverses[i])
    fars[1].wait_recv()
    inverse = far_scale(1)
    for k in range(9):
        lanes = pl.ds(128 * k, 128)
        totals = [
            home_sum[0, 0, :, lanes],
            home_sum[0, 1, :, lanes] + decoded(far_in[1, :, lanes], inverse),
        ]
        for half in range(2):
            column = k + 9 * half
            part, place = divmod(column, 5)
            for i in range(GROUP):
                row = 24 * half + SLAB * (i % 2)
                back = vis_sum[1, i, pl.ds(SLAB * part, SLAB), pl.ds(128 * place, 128)]
                out[:, i, pl.ds(128 * column, 128)] = totals[i // 2][row : row + SLAB] + back

    for copy in far_copies + sib_copies + relays + sent:
        copy.wait_send()


def solution(mesh):
    small, large, along_x, screened = tables()
    any_space = pl.BlockSpec(memory_space=pl.ANY)
    bf16, f32 = jnp.bfloat16, jnp.float32
    dma = pltpu.SemaphoreType.DMA
    call = pl.pallas_call(
        kernel,
        out_shape=pltpu.VMEM((SLAB, GROUP, PLANE), f32),
        in_specs=[pl.BlockSpec(memory_space=pltpu.VMEM)] + [any_space] * 4,
        out_specs=pl.BlockSpec(memory_space=pltpu.VMEM),
        scratch_shapes=[
            pltpu.VMEM((18, POINTS, 128), f32),
            pltpu.VMEM((5, ROWS, 128), f32),
            pltpu.VMEM((GROUP, POINTS, 640), bf16),
            pltpu.VMEM((4, 2, POINTS, PLANE // 2), bf16),
            pltpu.VMEM((2, 4, POINTS, 640), bf16),
            pltpu.VMEM((2, 4, POINTS, PLANE // 2), f32),
            pltpu.VMEM((ROWS, PLANE), bf16),
            pltpu.VMEM((ROWS, PLANE), bf16),
            pltpu.VMEM((ROWS, PLANE), bf16),
            pltpu.VMEM((ROWS, PLANE), bf16),
            pltpu.VMEM((ROWS, PLANE), f32),
            pltpu.VMEM((4, 2, POINTS, PLANE // 2), f32),
            pltpu.VMEM((4, POINTS, PLANE // 2), f32),
            pltpu.VMEM((2, 4, POINTS, 640), f32),
            pltpu.VMEM((2, 4, POINTS, 640), bf16),
            pltpu.VMEM((2, POINTS, PLANE // 2), f32),
            pltpu.VMEM((2, POINTS, PLANE // 2), f32),
            pltpu.VMEM((POINTS, PLANE // 2), f32),
            pltpu.VMEM((2, POINTS, PLANE // 2 + 128), bf16),
            pltpu.VMEM((2, POINTS, PLANE // 2 + 128), bf16),
            pltpu.VMEM((2, 4, POINTS, 640), bf16),
            pltpu.VMEM(small.shape, bf16),
            pltpu.VMEM(large.shape, bf16),
            pltpu.VMEM(along_x.shape[1:], bf16),
            pltpu.VMEM(screened.shape, f32),
            dma((4,)), dma((4, 2)), dma((4, 2)), dma((2, 4)), dma((2, 4)),
            dma((2, 3)), dma((2, 3)), dma((2, 4)), dma((2, 4)),
        ],
        compiler_params=pltpu.CompilerParams(
            collective_id=0, has_side_effects=True, vmem_limit_bytes=60 << 20
        ),
    )

    def body(orbitals):
        return -MIXING * jnp.transpose(
            call(jnp.transpose(orbitals, (1, 0, 2)), small, large, along_x, screened), (1, 0, 2)
        )

    placed = P("band", "grid", None)
    return jax.shard_map(
        body, mesh=mesh, in_specs=(placed,), out_specs=placed, check_vma=False
    )
```

```python
import functools

import jax
import jax.numpy as jnp
import ml_dtypes
import numpy as np
from jax import lax
from jax.experimental import pallas as pl
from jax.experimental.pallas import tpu as pltpu
from jax.sharding import PartitionSpec as P

POINTS = 48
PLANE = POINTS * POINTS
GROUP = 4
SLAB = 12
BAND = 64
CHUNK = 384
BOX = 37.25
OMEGA = 0.106
MIXING = 0.25
ROWS = 4 * GROUP * SLAB
HALF = ROWS // 2
BEHIND = (-1, 2)
CLASSES = ((0, 384), (384, 384), (768, 768), (1536, 768))


def halves(table):
    high = table.astype(ml_dtypes.bfloat16)
    low = (table - high.astype(np.float64)).astype(ml_dtypes.bfloat16)
    return high, low


def tables():
    index = np.arange(POINTS)
    angles = 2.0 * np.pi * (np.outer(index, index) % POINTS) / POINTS
    cas = np.cos(angles) + np.sin(angles)

    def spread(weights):
        rows = np.zeros((8, POINTS))
        for fine in range(8):
            rows[fine, fine::8] = weights
        return rows

    even, odd = [1, 1, 1, 1, 1, 1], [1, -1, 1, -1, 1, -1]
    real2, imag2 = [1, -0.5, -0.5, 1, -0.5, -0.5], [0, 1, -1, 0, 1, -1]
    real1, imag1 = [1, 0.5, -0.5, -1, -0.5, 0.5], [0, 1, 1, 0, -1, -1]
    matrices, order = [], []
    for parts, residues in (
        ((even,), (0,)),
        ((odd,), (3,)),
        ((real2, imag2), (2, 4)),
        ((real1, imag1), (1, 5)),
    ):
        folded = np.concatenate([spread(part) for part in parts])
        waves = [k for k in range(POINTS) if k % 6 in residues]
        small = cas[waves] @ folded.T @ np.linalg.inv(folded @ folded.T)
        matrices.append(np.kron(small, cas))
        order += waves
    signed = ((index + POINTS // 2) % POINTS - POINTS // 2) * (2.0 * np.pi / BOX)
    along_y, along_z = np.repeat(np.array(order), POINTS), np.tile(index, POINTS)
    squares = (
        signed[:, None] ** 2 + signed[along_y][None] ** 2 + signed[along_z][None] ** 2
    )
    bounded = np.where(squares > 0.0, squares, 1.0)
    screened = 4.0 * np.pi / bounded * (1.0 - np.exp(-bounded / (4.0 * OMEGA * OMEGA)))
    screened = np.where(squares > 0.0, screened, np.pi / (OMEGA * OMEGA)) / POINTS**3

    forward = [halves(m.T) for m in matrices]
    inverse = [halves(m) for m in matrices]
    small = np.stack([np.stack([w[c][p] for c in (0, 1) for p in (0, 1)]) for w in (forward, inverse)])
    large = np.stack([np.stack([w[c][p] for c in (2, 3) for p in (0, 1)]) for w in (forward, inverse)])

    along = []
    for device in range(4):
        matrix = np.zeros((2, POINTS, 4, 2, SLAB))
        for slot in range(4):
            base = SLAB * (device ^ slot)
            for orbital in range(2):
                matrix[orbital, :, slot, orbital, :] = cas[:, base : base + SLAB]
        matrix = matrix.reshape(HALF, HALF)
        for source in (matrix, matrix.T):
            high, low = halves(source)
            top = np.concatenate([high, high], axis=1)
            bottom = np.concatenate([low, np.zeros_like(low)], axis=1)
            along.append(np.concatenate([top, bottom], axis=0))
    along_x = np.stack(along).reshape(4, 2, ROWS, ROWS)
    return small, large, along_x, screened.astype(np.float32)


def parted(value):
    high = value.astype(jnp.bfloat16)
    return high, (value - high.astype(jnp.float32)).astype(jnp.bfloat16)


def dot(left, right):
    return jnp.dot(left, right, preferred_element_type=jnp.float32)


def fold(d):
    s = [d[p] + d[p + 3] for p in range(3)]
    t = [d[p] - d[p + 3] for p in range(3)]
    u, v = s[1] + s[2], t[1] - t[2]
    return (s[0] + u, t[0] - v, s[0] - 0.5 * u, s[1] - s[2], t[0] + 0.5 * v, t[1] + t[2])


def unfold(f):
    z0, z3, r2, i2, r1, i1 = f
    a, b = z0 - 0.5 * r2, z3 - 0.5 * r1
    s = (z0 + r2, a + i2, a - i2)
    t = (z3 + r1, i1 - b, i1 + b)
    return [s[p] + t[p] for p in range(3)] + [s[p] - t[p] for p in range(3)]


def densities(pair, two, home_in, wide, z_hi, z_lo):
    for tile in range(3):
        d = [None] * 6
        for p in range(3):
            lanes = pl.ds(p * CHUNK + tile * 128, 128)
            values = [
                home_in[2 * pair + k, two, :, lanes].astype(jnp.float32) * wide[2 * pair + k, :, lanes]
                for k in range(2)
            ]
            d[p] = jnp.concatenate([value[:24] for value in values], axis=0)
            d[p + 3] = jnp.concatenate([value[24:] for value in values], axis=0)
        for p, value in enumerate(fold(d)):
            at = (pl.ds(HALF * two + POINTS * pair, POINTS), pl.ds(p * CHUNK + tile * 128, 128))
            z_hi[at], z_lo[at] = parted(value)


def weights(small, large, which, cls):
    return (small, large)[cls // 2], which, 2 * (cls % 2)


def plane(two, cls, source, table):
    ref, which, base = table
    first, lanes = CLASSES[cls]
    high, low = (part[pl.ds(HALF * two, HALF), pl.ds(first, lanes)] for part in source)
    both = dot(jnp.concatenate([high, low], axis=0), ref[which, base])
    return both[:HALF] + both[HALF:] + dot(high, ref[which, base + 1])


def middle(start, two, s, u, along_x, screened):
    at = (pl.ds(HALF * two, HALF), pl.ds(start, 768))
    table = screened[:, pl.ds(start, 768)]
    both = dot(along_x[0], jnp.concatenate([s[0][at], s[1][at]], axis=0))
    weighted = (both[:HALF] + both[HALF:]) * jnp.concatenate([table] * 2, axis=0)
    both = dot(along_x[1], jnp.concatenate(parted(weighted), axis=0))
    u[0][at], u[1][at] = parted(both[:HALF] + both[HALF:])


def products(q, two, last, home_in, wide, g, home_sum, vis_part, vis_sum):
    for tile in range(3):
        f = [g[pl.ds(HALF * two + 24 * q, 24), pl.ds(p * CHUNK + tile * 128, 128)] for p in range(6)]
        values = unfold(f)
        for p in range(3):
            lanes = pl.ds(p * CHUNK + tile * 128, 128)
            value = jnp.concatenate([values[p], values[p + 3]], axis=0)
            home = value * wide[q, :, lanes]
            if last:
                home = home + home_sum[q, two, :, lanes]
            home_sum[q, two, :, lanes] = home
            other = value * home_in[q, two, :, lanes].astype(jnp.float32)
            if two == 0:
                vis_part[q, :, lanes] = other
                continue
            other = other + vis_part[q, :, lanes]
            for half in range(2):
                rows = other[24 * half : 24 * half + SLAB] + other[24 * half + SLAB : 24 * half + 24]
                part, place = divmod(9 * half + 3 * p + tile, 5)
                vis_sum[q, pl.ds(SLAB * part, SLAB), pl.ds(128 * place, 128)] = rows


def scale_of(values):
    top = functools.reduce(jnp.maximum, [jnp.max(jnp.abs(v), axis=0, keepdims=True) for v in values])
    top = jnp.max(top, axis=1, keepdims=True)
    return (220.0 / jnp.maximum(top, 1e-30)).astype(jnp.bfloat16).astype(jnp.float32)


def coded(value, scale):
    power = value * scale
    for _ in range(4):
        power = power * power
    return jnp.where(value < 0.0, -power, power).astype(jnp.bfloat16)


def decoded(code, inverse):
    power = code.astype(jnp.float32)
    value = jnp.exp2(jnp.log2(jnp.abs(power)) * 0.0625) * inverse
    return jnp.where(power < 0.0, -value, value)


def code_visitor(source, target):
    tiles = [source[:, pl.ds(128 * k, 128)] for k in range(5)]
    scale = scale_of(tiles)
    spare = lax.broadcasted_iota(jnp.int32, (POINTS, 128), 0) >= 3 * SLAB
    for k in range(5):
        code = coded(tiles[k], scale)
        if k >= 3:
            code = jnp.where(spare, jnp.broadcast_to(scale, (POINTS, 128)), code.astype(jnp.float32))
        target[:, pl.ds(128 * k, 128)] = code.astype(jnp.bfloat16)


def kernel(
    arrived_hbm, small_hbm, large_hbm, along_hbm, screened_hbm, out,
    arrived, spread_rows, spread_parts, orbitals, home_in, vis_in, wide, z_hi, z_lo, s_hi, s_lo, g,
    home_sum, vis_part, vis_sum, vis_code, sib_relay, sib_final, far_sum, far_out, far_in, vis_back,
    small, large, along_x, screened,
    table_sem, home_send, home_recv, vis_send, vis_recv,
    sum_send, sum_recv, back_send, back_recv,
):
    band, me = lax.axis_index("band"), lax.axis_index("grid")

    def partner(bit):
        return me + bit - 2 * bit * (lax.rem(me // bit, 2))

    def group(distance):
        return lax.rem(band + distance + BAND, BAND)

    def xor(a, j):
        low = lax.rem(a + j, 2)
        high = lax.rem(a // 2 + j // 2, 2)
        return 2 * high + low

    sibling, far = (band, partner(1)), (band, partner(2))

    barrier = pltpu.get_barrier_semaphore()
    pl.semaphore_signal(barrier, 1, device_id=sibling)
    pl.semaphore_signal(barrier, 1, device_id=far)
    for distance in BEHIND:
        for j in range(4):
            pl.semaphore_signal(barrier, 1, device_id=(group(-distance), j))

    entry = pltpu.make_async_copy(arrived_hbm, arrived, table_sem.at[4])
    entry.start()
    loads = [
        pltpu.make_async_copy(small_hbm, small, table_sem.at[0]),
        pltpu.make_async_copy(large_hbm, large, table_sem.at[1]),
        pltpu.make_async_copy(along_hbm.at[me], along_x, table_sem.at[2]),
        pltpu.make_async_copy(screened_hbm, screened, table_sem.at[3]),
    ]
    spread_parts[3:5] = jnp.zeros((2, ROWS, 128), jnp.float32)
    entry.wait()
    for k in range(18):
        part, place = divmod(k, 5)
        for r in range(SLAB):
            value = arrived[r, :, pl.ds(128 * k, 128)].astype(jnp.float32)
            spread_rows[k, pl.ds(r, GROUP, stride=SLAB), :] = value
            spread_parts[place, pl.ds(SLAB * part + r, GROUP, stride=POINTS), :] = value
    for i in range(GROUP):
        for place in range(5):
            orbitals[i, :, pl.ds(128 * place, 128)] = spread_parts[
                place, pl.ds(POINTS * i, POINTS), :
            ].astype(jnp.bfloat16)
    for two in range(2):
        for k in range(9):
            value = jnp.concatenate(
                [spread_rows[k + 9 * half, pl.ds(24 * two, 24), :] for half in range(2)], axis=0
            )
            home_in[0, two, :, pl.ds(128 * k, 128)] = value.astype(jnp.bfloat16)
    vis_sum[:, :, pl.ds(32, 16), pl.ds(384, 256)] = jnp.zeros((2, 4, 16, 256), jnp.float32)
    pl.semaphore_wait(barrier, 10)

    def home_copy(source, slot, two, target):
        copy = pltpu.make_async_remote_copy(
            home_in.at[source, two],
            home_in.at[slot, two],
            home_send.at[slot, two],
            home_recv.at[slot, two],
            device_id=target,
        )
        copy.start()
        return copy

    sent = []

    def send_visitors(s):
        for j in range(4):
            copy = pltpu.make_async_remote_copy(
                orbitals.at[j],
                vis_in.at[s, xor(me, j)],
                vis_send.at[s, j],
                vis_recv.at[s, xor(me, j)],
                device_id=(group(BEHIND[s]), j),
            )
            copy.start()
            sent.append(copy)

    sib_copies = [home_copy(0, 1, 0, sibling)]
    send_visitors(0)
    far_copies = [home_copy(0, 2, 0, far)]
    sib_copies.append(home_copy(0, 1, 1, sibling))
    far_copies.append(home_copy(0, 2, 1, far))
    send_visitors(1)

    for load in loads:
        load.start()

    def widen(s, slots):
        for q in slots:
            pltpu.make_async_remote_copy(
                orbitals.at[0], vis_in.at[s, q], vis_send.at[s, 0], vis_recv.at[s, q],
                device_id=sibling,
            ).wait_recv()
            for place in range(5):
                value = vis_in[s, q, :, pl.ds(128 * place, 128)].astype(jnp.float32)
                for part in range(4 if place < 3 else 3):
                    half, k = divmod(5 * part + place, 9)
                    rows = value[SLAB * part : SLAB * part + SLAB]
                    for copy in range(2):
                        wide[s, q, pl.ds(24 * half + SLAB * copy, SLAB), pl.ds(128 * k, 128)] = rows

    def forward(two):
        for cls in range(4):
            first, lanes = CLASSES[cls]
            at = (pl.ds(HALF * two, HALF), pl.ds(first, lanes))
            value = plane(two, cls, (z_hi, z_lo), weights(small, large, 0, cls))
            s_hi[at], s_lo[at] = parted(value)

    def backward(two):
        for cls in range(4):
            first, lanes = CLASSES[cls]
            at = (pl.ds(HALF * two, HALF), pl.ds(first, lanes))
            g[at] = plane(two, cls, (s_hi, s_lo), weights(small, large, 1, cls))

    def across(two):
        for start in range(0, PLANE, 768):
            middle(start, two, (s_hi, s_lo), (s_hi, s_lo), along_x, screened)

    def slab(q, two, s):
        products(q, two, s == 1, home_in, wide.at[s], g, home_sum, vis_part, vis_sum.at[s])

    def send_back(s, q):
        code_visitor(vis_sum.at[s, q], vis_code.at[s, q])
        copy = pltpu.make_async_remote_copy(
            vis_code.at[s, q],
            vis_back.at[s, me],
            back_send.at[s, q],
            back_recv.at[s, me],
            device_id=(group(-BEHIND[s]), xor(me, q)),
        )
        copy.start()
        sent.append(copy)

    def sum_copy(source, target_ref, two, kind, target):
        copy = pltpu.make_async_remote_copy(
            source, target_ref, sum_send.at[two, kind], sum_recv.at[two, kind], device_id=target
        )
        copy.start()
        sent.append(copy)
        return copy

    columns = [pl.ds(128 * k, 128) for k in range(9)]

    def to_far(two, relayed):
        relayed.wait_recv()
        for lanes in columns:
            far_sum[:, lanes] = home_sum[2, two, :, lanes] + sib_relay[two, :, lanes]
        scale = scale_of([far_sum[:, lanes] for lanes in columns])
        for lanes in columns:
            far_out[two, :, lanes] = coded(far_sum[:, lanes], scale)
        far_out[two, :, pl.ds(PLANE // 2, 128)] = jnp.broadcast_to(scale, (POINTS, 128)).astype(jnp.bfloat16)
        return sum_copy(far_out.at[two], far_in.at[two], two, 1, far)

    sib_copies[0].wait_recv()
    widen(0, (0, 1))
    densities(0, 0, home_in, wide.at[0], z_hi, z_lo)
    far_copies[0].wait_recv()
    relays = [home_copy(2, 3, 0, sibling)]
    widen(0, (2, 3))
    relays[0].wait_recv()
    densities(1, 0, home_in, wide.at[0], z_hi, z_lo)
    for load in loads:
        load.wait()
    forward(0)
    across(0)
    backward(0)
    far_copies[1].wait_recv()
    relays.append(home_copy(2, 3, 1, sibling))
    for q in range(4):
        slab(q, 0, 0)

    sib_copies[1].wait_recv()
    densities(0, 1, home_in, wide.at[0], z_hi, z_lo)
    relays[1].wait_recv()
    densities(1, 1, home_in, wide.at[0], z_hi, z_lo)
    forward(1)
    across(1)
    backward(1)
    for q in (2, 3, 0, 1):
        slab(q, 1, 0)
        send_back(0, q)

    widen(1, range(4))
    for pair in range(2):
        densities(pair, 0, home_in, wide.at[1], z_hi, z_lo)
    forward(0)
    across(0)
    backward(0)
    slab(3, 0, 1)
    relayed = sum_copy(home_sum.at[3, 0], sib_relay.at[0], 0, 0, sibling)
    slab(2, 0, 1)
    slab(1, 0, 1)
    finals = [sum_copy(home_sum.at[1, 0], sib_final.at[0], 0, 2, sibling)]
    slab(0, 0, 1)

    for pair in range(2):
        densities(pair, 1, home_in, wide.at[1], z_hi, z_lo)
    fars = [to_far(0, relayed)]
    forward(1)
    across(1)
    backward(1)
    slab(3, 1, 1)
    relayed = sum_copy(home_sum.at[3, 1], sib_relay.at[1], 1, 0, sibling)
    send_back(1, 3)
    slab(2, 1, 1)
    send_back(1, 2)
    fars.append(to_far(1, relayed))
    slab(1, 1, 1)
    finals.append(sum_copy(home_sum.at[1, 1], sib_final.at[1], 1, 2, sibling))
    slab(0, 1, 1)
    send_back(1, 1)
    send_back(1, 0)

    def returned(s):
        for j in range(4):
            pltpu.make_async_remote_copy(
                vis_code.at[s, 0], vis_back.at[s, j], back_send.at[s, 0], back_recv.at[s, j],
                device_id=sibling,
            ).wait_recv()
        return [
            1.0 / vis_back[s, i, pl.ds(32, 16), pl.ds(384, 128)].astype(jnp.float32)[15:] for i in range(4)
        ]

    def far_scale(two):
        return 1.0 / far_in[two, pl.ds(0, 16), pl.ds(PLANE // 2, 128)].astype(jnp.float32)[:1]

    finals[0].wait_recv()
    fars[0].wait_recv()
    inverse = far_scale(0)
    for lanes in columns:
        home_sum[0, 0, :, lanes] = (
            home_sum[0, 0, :, lanes] + sib_final[0, :, lanes] + decoded(far_in[0, :, lanes], inverse)
        )
    inverses = returned(0)
    for i in range(GROUP):
        for place in range(5):
            lanes = pl.ds(128 * place, 128)
            vis_sum[1, i, :, lanes] = decoded(vis_back[0, i, :, lanes], inverses[i])
    finals[1].wait_recv()
    for lanes in columns:
        home_sum[0, 1, :, lanes] = home_sum[0, 1, :, lanes] + sib_final[1, :, lanes]
    inverses = returned(1)
    for i in range(GROUP):
        for place in range(5):
            lanes = pl.ds(128 * place, 128)
            vis_sum[1, i, :, lanes] = vis_sum[1, i, :, lanes] + decoded(vis_back[1, i, :, lanes], inverses[i])
    fars[1].wait_recv()
    inverse = far_scale(1)
    for k in range(9):
        lanes = pl.ds(128 * k, 128)
        totals = [
            home_sum[0, 0, :, lanes],
            home_sum[0, 1, :, lanes] + decoded(far_in[1, :, lanes], inverse),
        ]
        for half in range(2):
            column = k + 9 * half
            part, place = divmod(column, 5)
            for i in range(GROUP):
                row = 24 * half + SLAB * (i % 2)
                back = vis_sum[1, i, pl.ds(SLAB * part, SLAB), pl.ds(128 * place, 128)]
                out[:, i, pl.ds(128 * column, 128)] = totals[i // 2][row : row + SLAB] + back

    for copy in far_copies + sib_copies + relays + sent:
        copy.wait_send()


def solution(mesh):
    small, large, along_x, screened = tables()
    any_space = pl.BlockSpec(memory_space=pl.ANY)
    bf16, f32 = jnp.bfloat16, jnp.float32
    dma = pltpu.SemaphoreType.DMA
    call = pl.pallas_call(
        kernel,
        out_shape=pltpu.VMEM((SLAB, GROUP, PLANE), f32),
        in_specs=[any_space] * 5,
        out_specs=pl.BlockSpec(memory_space=pltpu.VMEM),
        scratch_shapes=[
            pltpu.VMEM((SLAB, GROUP, PLANE), bf16),
            pltpu.VMEM((18, POINTS, 128), f32),
            pltpu.VMEM((5, ROWS, 128), f32),
            pltpu.VMEM((GROUP, POINTS, 640), bf16),
            pltpu.VMEM((4, 2, POINTS, PLANE // 2), bf16),
            pltpu.VMEM((2, 4, POINTS, 640), bf16),
            pltpu.VMEM((2, 4, POINTS, PLANE // 2), f32),
            pltpu.VMEM((ROWS, PLANE), bf16),
            pltpu.VMEM((ROWS, PLANE), bf16),
            pltpu.VMEM((ROWS, PLANE), bf16),
            pltpu.VMEM((ROWS, PLANE), bf16),
            pltpu.VMEM((ROWS, PLANE), f32),
            pltpu.VMEM((4, 2, POINTS, PLANE // 2), f32),
            pltpu.VMEM((4, POINTS, PLANE // 2), f32),
            pltpu.VMEM((2, 4, POINTS, 640), f32),
            pltpu.VMEM((2, 4, POINTS, 640), bf16),
            pltpu.VMEM((2, POINTS, PLANE // 2), f32),
            pltpu.VMEM((2, POINTS, PLANE // 2), f32),
            pltpu.VMEM((POINTS, PLANE // 2), f32),
            pltpu.VMEM((2, POINTS, PLANE // 2 + 128), bf16),
            pltpu.VMEM((2, POINTS, PLANE // 2 + 128), bf16),
            pltpu.VMEM((2, 4, POINTS, 640), bf16),
            pltpu.VMEM(small.shape, bf16),
            pltpu.VMEM(large.shape, bf16),
            pltpu.VMEM(along_x.shape[1:], bf16),
            pltpu.VMEM(screened.shape, f32),
            dma((5,)), dma((4, 2)), dma((4, 2)), dma((2, 4)), dma((2, 4)),
            dma((2, 3)), dma((2, 3)), dma((2, 4)), dma((2, 4)),
        ],
        compiler_params=pltpu.CompilerParams(
            collective_id=0, has_side_effects=True, vmem_limit_bytes=60 << 20
        ),
    )

    def body(orbitals):
        return -MIXING * jnp.transpose(
            call(jnp.transpose(orbitals, (1, 0, 2)), small, large, along_x, screened), (1, 0, 2)
        )

    placed = P("band", "grid", None)
    return jax.shard_map(
        body, mesh=mesh, in_specs=(placed,), out_specs=placed, check_vma=False
    )
```
